32 devices in a mesh: dp: 4 (over y, x), fsdp: 8 (over z, core).
Axes of the slice: x: 2, y: 2, z: 4, core: 2. Of those that a mesh axis runs over, the one named last changes fastest.
Arguments:
- hidden_in: bfloat16 [8, 1024, 1536], P('dp', 'fsdp'), may hold values from -6 to 6
- doc_lengths: int32 [8, 1], P('dp'), may hold values from 0 to 1024, as said below
- norm_gain: bfloat16 [2, 1536], P(None, 'fsdp'), may hold values from 0.5 to 1.5
- input_proj: bfloat16 [2, 1536, 6400], P(None, 'fsdp'), may hold values from -0.15625 to 0.15625
- step_proj: bfloat16 [2, 48, 1536], P(None, None, 'fsdp'), may hold values from -0.15625 to 0.15625
- conv_weight: bfloat16 [2, 4, 3328], P(None, None, 'fsdp'), may hold values from -3 to 3
- conv_bias: bfloat16 [2, 3328], P(None, 'fsdp'), may hold values from -3 to 3
- step_bias: bfloat16 [2, 48], P(None, 'fsdp'), may hold values from -10.5 to -2.9
- decay_log: bfloat16 [2, 48], P(None, 'fsdp'), may hold values from 0 to 0.69921875
- skip_gain: bfloat16 [2, 48], P(None, 'fsdp'), may hold values from 0.5 to 1.5
- gate_gain: bfloat16 [2, 3072], P(None, 'fsdp'), may hold values from 0.5 to 1.5
- output_proj: bfloat16 [2, 3072, 1536], P(None, 'fsdp'), may hold values from -0.109375 to 0.109375
- cotangent: bfloat16 [8, 1024, 1536], P('dp', 'fsdp'), may hold values from -6 to 6
Outputs:
- hidden_out: bfloat16 [8, 1024, 1536], P('dp', 'fsdp')
- hidden_grad: float32 [8, 1024, 1536], P('dp', 'fsdp')
- norm_gain_grad: float32 [2, 1536], P(None, 'fsdp')
- input_proj_grad: float32 [2, 1536, 6400], P(None, 'fsdp')
- step_proj_grad: float32 [2, 48, 1536], P(None, None, 'fsdp')
- conv_weight_grad: float32 [2, 4, 3328], P(None, None, 'fsdp')
- conv_bias_grad: float32 [2, 3328], P(None, 'fsdp')
- step_bias_grad: float32 [2, 48], P(None, 'fsdp')
- decay_log_grad: float32 [2, 48], P(None, 'fsdp')
- skip_gain_grad: float32 [2, 48], P(None, 'fsdp')
- gate_gain_grad: float32 [2, 3072], P(None, 'fsdp')
- output_proj_grad: float32 [2, 3072, 1536], P(None, 'fsdp')
The draws below stay inside these ranges and needn't reach their ends.
Inputs may be any that keep to these rules, and one draw needn't show every extreme that they name: `doc_lengths`: row r lists the documents of packed sequence r in order: its entries sum to 1024, each entry is 0 or at least 1024, the first is not 0; of the 2 rows of each index of dp at least one holds a single document.
All inputs are finite; a program needn't handle non-finite values.
Results may differ from the reference program's by a relative error of at most 0.022.
Values may be sent and summed in bfloat16 or wider, within the bound.
No kernel may reach another device: no remote copies, remote signals or barrier semaphores. Data moves between devices by JAX's collectives and lax.ppermute only.
A program may use at most 384 MiB of HBM per device.

```python
import math
import jax
import jax.numpy as jnp
from jax import lax

D = 1536
INNER = 3072
HEADS = 48
HEAD_DIM = 64
STATE = 128
CONV = 4
LAYERS = 2
MIN_DOC = 1024
MB = 2
TOK_MB = 128
PROJ = 6400
CONV_CH = 3328
ROW_LEN = 1024
ROWS = 8
SLOTS = 1


def draw_doc_lengths(key, part):
    key = jax.random.fold_in(key, 7)
    active_key, weight_key, whole_key = jax.random.split(key, 3)
    slot_ids = jnp.arange(SLOTS, dtype=jnp.int32)
    row_ids = jnp.arange(ROWS, dtype=jnp.int32)
    active = jax.random.randint(active_key, (ROWS, SLOTS), 0, 2)
    active = jnp.maximum(active, (slot_ids[None, :] == 0).astype(jnp.int32))
    whole_row = jax.random.randint(whole_key, (ROWS // MB,), 0, MB)
    single = row_ids == row_ids // MB * MB + whole_row[row_ids // MB]
    active = jnp.where(single[:, None], (slot_ids[None, :] == 0).astype(jnp.int32), active)
    doc_count = jnp.sum(active, axis=1, keepdims=True)
    spare_len = ROW_LEN - doc_count * MIN_DOC
    weights = jax.random.randint(weight_key, (ROWS, SLOTS), 1, 16) * active
    extra_len = spare_len * weights // jnp.sum(weights, axis=1, keepdims=True)
    leftover = spare_len - jnp.sum(extra_len, axis=1, keepdims=True)
    extra_len = extra_len + leftover * (slot_ids[None, :] == 0).astype(jnp.int32)
    return (active * MIN_DOC + extra_len).astype(jnp.int32)


def draw_step_bias(key, part):
    key = jax.random.fold_in(key, 11)
    pick_key, slow_key, fast_key = jax.random.split(key, 3)
    slow_share = 0.5
    slow_mask = jax.random.uniform(pick_key, (LAYERS, HEADS)) < slow_share
    slow_step = jnp.exp(jax.random.uniform(slow_key, (LAYERS, HEADS), minval=math.log(3e-05), maxval=math.log(0.00015)))
    fast_step = jnp.exp(jax.random.uniform(fast_key, (LAYERS, HEADS), minval=math.log(0.01), maxval=math.log(0.05)))
    step_size = jnp.where(slow_mask, slow_step, fast_step).astype(jnp.float32)
    return jnp.log(jnp.expm1(step_size)).astype(jnp.bfloat16)


def shard_levels(stream_key, shape, cuts, low, top_value):
    def one(dim, parts):
        draws = jax.random.uniform(jax.random.fold_in(jax.random.fold_in(stream_key, 6), dim), (parts,), jnp.float32, low / len(cuts), top_value / len(cuts))
        return jnp.repeat(jnp.exp(draws), shape[dim] // parts).reshape((-1,) + (1,) * (len(shape) - dim - 1))

    level = one(*cuts[0])
    for cut in cuts[1:]:
        level = level * one(*cut)
    return level


def centred(rng, extent, deviation, most, shards=(), held_as=jnp.bfloat16):
    level = shard_levels(rng, extent, shards, -0.22, 0.18) if shards else 1.0
    values = jax.random.normal(rng, extent, jnp.float32) * deviation * level
    return jnp.minimum(jnp.maximum(values, -most), most).astype(held_as)


def setup_inputs(seed: int = 0) -> dict:
    key_of = jax.random.split(jax.random.key(seed), 14)
    return {
        "hidden_in": centred(key_of[0], (ROWS, ROW_LEN, D), 1.0, 6.0, ((0, 4), (1, 8))),
        "doc_lengths": draw_doc_lengths(jax.random.fold_in(key_of[13], 71), 0),
        "norm_gain": jnp.clip(1.0 + 0.1 * jax.random.normal(key_of[2], (LAYERS, D), jnp.float32), 0.5, 1.5).astype(jnp.bfloat16),
        "input_proj": centred(key_of[3], (LAYERS, D, PROJ), D ** -0.5, 0.15625, ((1, 8),)),
        "step_proj": centred(key_of[4], (LAYERS, HEADS, D), D ** -0.5, 0.15625, ((2, 8),)),
        "conv_weight": centred(key_of[5], (LAYERS, CONV, CONV_CH), CONV ** -0.5, 3.0, ((2, 8),)),
        "conv_bias": centred(key_of[6], (LAYERS, CONV_CH), 0.5, 3.0, ((1, 8),)),
        "step_bias": draw_step_bias(jax.random.fold_in(key_of[13], 71), 0),
        "decay_log": jnp.clip(0.69921875 * jax.random.uniform(key_of[8], (LAYERS, HEADS), jnp.float32) ** shard_levels(key_of[8], (LAYERS, HEADS), ((1, 8),), -0.2, 0.2), 0.0, 0.69921875).astype(jnp.bfloat16),
        "skip_gain": jnp.clip(0.5 + 1.0 * jax.random.uniform(key_of[9], (LAYERS, HEADS), jnp.float32) ** shard_levels(key_of[9], (LAYERS, HEADS), ((1, 8),), -0.2, 0.2), 0.5, 1.5).astype(jnp.bfloat16),
        "gate_gain": jnp.clip(1.0 + 0.1 * jax.random.normal(key_of[10], (LAYERS, INNER), jnp.float32), 0.5, 1.5).astype(jnp.bfloat16),
        "output_proj": centred(key_of[11], (LAYERS, INNER, D), INNER ** -0.5, 0.109375, ((1, 8),)),
        "cotangent": centred(key_of[12], (ROWS, ROW_LEN, D), 1.0, 6.0, ((0, 4), (1, 8))),
    }


EPSILON = 1e-05
HIGHEST = lax.Precision.HIGHEST

@jax.custom_vjp
def low(v):
    return lax.optimization_barrier(v.astype(jnp.bfloat16)).astype(jnp.float32)

@jax.custom_vjp
def low_back(v):
    return v

def low_keep(v):
    return (low(v), None)

def low_pass(kept, grad):
    return (grad,)

def back_keep(v):
    return (v, None)

def back_low(kept, grad):
    return (low(grad),)
low.defvjp(low_keep, low_pass)
low_back.defvjp(back_keep, back_low)

def rms_scale(values, weight):
    inverse_rms = lax.rsqrt(lax.optimization_barrier(jnp.mean(values * values, axis=-1, keepdims=True)) + EPSILON)
    return values * inverse_rms * weight

def gate_norm(ssd_out, gate_row, weight):
    return rms_scale(ssd_out * jax.nn.silu(gate_row), weight)

def segment_ids(lengths_row, positions):
    doc_ends = jnp.cumsum(lengths_row).astype(jnp.int32)
    return lax.optimization_barrier(jnp.sum((doc_ends[None, :] <= positions[:, None]).astype(jnp.int32), axis=1)).astype(jnp.int32)

def convolve(conv_in, weight, bias_row, segment):
    row_count = conv_in.shape[0]
    padded = jnp.pad(conv_in, ((CONV - 1, 0), (0, 0)))
    segment_pad = jnp.pad(segment, (CONV - 1, 0), constant_values=-1)
    summed = jnp.zeros(conv_in.shape, jnp.float32) + bias_row[None, :]
    for offset in range(CONV):
        same_doc = (segment_pad[offset:offset + row_count] == segment)[:, None]
        summed = summed + weight[offset][None, :] * jnp.where(same_doc, padded[offset:offset + row_count], 0.0)
    return jax.nn.silu(summed)

def split_inputs(xbc):
    row_count = xbc.shape[0]
    values = xbc[:, :INNER].reshape(row_count, HEADS, HEAD_DIM)
    writers = xbc[:, INNER:INNER + STATE]
    readers = xbc[:, INNER + STATE:]
    return (values, writers, readers)

def decay_sums(step_raw, step_bias, decay_log):
    step_sizes = jax.nn.softplus(step_raw + step_bias[None, :])
    log_decay = jnp.cumsum(step_sizes * (-jnp.exp(decay_log))[None, :], axis=0)
    return (step_sizes, log_decay)

def summarize(xbc, step_raw, step_bias, decay_log, starts):
    values, writers, readers = split_inputs(xbc)
    step_sizes, log_decay = decay_sums(step_raw, step_bias, decay_log)
    row_count = xbc.shape[0]
    run_counts = jnp.cumsum(starts).astype(jnp.int32)
    live_mask = (run_counts == run_counts[-1]).astype(jnp.float32)
    weights = jnp.exp(log_decay[-1][None, :] - log_decay) * step_sizes * live_mask[:, None]
    scaled = (values * weights[:, :, None]).reshape(row_count, INNER)
    contrib = lax.dot_general(scaled, writers, (((0,), (0,)), ((), ())), precision=HIGHEST)
    decay_end = jnp.exp(log_decay[-1]) * (run_counts[-1] == 0).astype(jnp.float32)
    return (decay_end, contrib.reshape(HEADS, HEAD_DIM, STATE))

def respond(xbc, step_raw, step_bias, decay_log, skip_row, state_in, starts):
    values, writers, readers = split_inputs(xbc)
    step_sizes, log_decay = decay_sums(step_raw, step_bias, decay_log)
    row_count = xbc.shape[0]
    run_counts = jnp.cumsum(starts).astype(jnp.int32)
    positions = jnp.arange(row_count, dtype=jnp.int32)
    causal = (positions[:, None] >= positions[None, :]) & (run_counts[:, None] == run_counts[None, :])
    scores = jnp.dot(readers, writers.T, precision=HIGHEST)
    head_logs = log_decay.T
    log_gaps = jnp.where(causal[None], head_logs[:, :, None] - head_logs[:, None, :], 0.0)
    mixing = jnp.where(causal[None], jnp.exp(log_gaps), 0.0) * scores[None]
    scaled = values * step_sizes[:, :, None]
    inner_part = jnp.einsum('hts,shp->thp', mixing, scaled, precision=HIGHEST)
    entering = jnp.exp(log_decay) * (run_counts == 0).astype(jnp.float32)[:, None]
    carried = jnp.einsum('hpn,tn->thp', state_in, readers, precision=HIGHEST) * entering[:, :, None]
    summed = inner_part + carried + skip_row[None, :, None] * values
    return summed.reshape(row_count, INNER)

def scan_blocks(xbc, step_raw, step_bias, decay_log, skip_row, starts):
    block_count = xbc.shape[0] // TOK_MB
    blocks = (xbc.reshape(block_count, TOK_MB, CONV_CH), step_raw.reshape(block_count, TOK_MB, HEADS), starts.reshape(block_count, TOK_MB))

    def advance(carry, block):
        state_in, bias_row, decay_row, skip_vals = carry
        xbc_block, raw_block, start_block = block
        decay_end, contrib = summarize(xbc_block, raw_block, bias_row, decay_row, start_block)
        out_block = respond(xbc_block, raw_block, bias_row, decay_row, skip_vals, state_in, start_block)
        return ((decay_end[:, None, None] * state_in + contrib, bias_row, decay_row, skip_vals), out_block)
    initial = (jnp.zeros((HEADS, HEAD_DIM, STATE), jnp.float32), step_bias, decay_log, skip_row)
    _, outputs = lax.scan(jax.checkpoint(advance), initial, blocks)
    return outputs.reshape(xbc.shape[0], INNER)

def mixer_layer(tokens, params, segment, starts):
    norm_weight, proj_weight, step_weight, conv_weight, conv_bias, step_bias, decay_log, skip_gain, gate_weight, out_weight = params
    normed = low(rms_scale(tokens, norm_weight))
    mixed = low_back(jnp.dot(normed, proj_weight, precision=HIGHEST))
    step_raw = low_back(jnp.dot(normed, step_weight.T, precision=HIGHEST))
    xbc = low(convolve(mixed[:, INNER:], conv_weight, conv_bias, segment))
    ssd_out = scan_blocks(xbc, step_raw, step_bias, decay_log, skip_gain, starts)
    gated = low(gate_norm(ssd_out, mixed[:, :INNER], gate_weight))
    return tokens + low_back(jnp.dot(gated, out_weight, precision=HIGHEST))

def reference(hidden_in, doc_lengths, norm_gain, input_proj, step_proj, conv_weight, conv_bias, step_bias, decay_log, skip_gain, gate_gain, output_proj, cotangent):
    weights = tuple((entry.astype(jnp.float32) for entry in (norm_gain, input_proj, step_proj, conv_weight, conv_bias, step_bias, decay_log, skip_gain, gate_gain, output_proj)))

    def one_row(totals, row):
        tokens, lengths_row, upstream = row
        segment = segment_ids(lengths_row, jnp.arange(ROW_LEN, dtype=jnp.int32))
        starts = jnp.concatenate([jnp.zeros((1,), jnp.int32), (segment[1:] != segment[:-1]).astype(jnp.int32)])

        def stack_forward(inputs, params):
            for layer_index in range(LAYERS):
                inputs = mixer_layer(inputs, tuple((entry[layer_index] for entry in params)), segment, starts)
            return inputs
        result, pullback = jax.vjp(stack_forward, tokens.astype(jnp.float32), weights)
        token_grad, weight_grads = pullback(upstream.astype(jnp.float32))
        return (jax.tree.map(jnp.add, totals, weight_grads), (result.astype(jnp.bfloat16), token_grad))
    initial = jax.tree.map(jnp.zeros_like, weights)
    totals, (hidden_out, hidden_grad) = lax.scan(one_row, initial, (hidden_in, doc_lengths, cotangent))
    return (hidden_out, hidden_grad, totals[0], totals[1], totals[2], totals[3], totals[4], totals[5], totals[6], totals[7], totals[8], totals[9])
```

```python
from functools import partial

import jax
import jax.numpy as jnp
from jax import lax
from jax.experimental import pallas as pl
from jax.experimental.pallas import tpu as pltpu
from jax.sharding import Mesh
from jax.sharding import PartitionSpec as P

BF = jnp.bfloat16
F32 = jnp.float32
HIGHEST = lax.Precision.HIGHEST
EPSILON = 1e-05
HEAD_DIM = 64
STATE = 128
LANES = 128
CHUNK = 128
HALO = 8
FAR = -1e30
PLANE = ("z", "core")


def mm(a, b):
    return lax.dot_general(a, b, (((1,), (0,)), ((), ())), preferred_element_type=F32)


def mm_bt(a, b):
    return lax.dot_general(a, b, (((1,), (1,)), ((), ())), preferred_element_type=F32)


def mm_at(a, b):
    return lax.dot_general(a, b, (((0,), (0,)), ((), ())), preferred_element_type=F32)


def mm_exact(a, b):
    return lax.dot_general(
        a, b, (((1,), (0,)), ((), ())), precision=HIGHEST, preferred_element_type=F32
    )


def iota2(shape, dim):
    return lax.broadcasted_iota(jnp.int32, shape, dim)


def head_spread(width):
    return (iota2((LANES, width), 1) // HEAD_DIM == iota2((LANES, width), 0)).astype(F32)


def head_gather(width):
    return (iota2((width, LANES), 0) // HEAD_DIM == iota2((width, LANES), 1)).astype(BF)


def softplus(x):
    return jnp.maximum(x, 0.0) + jnp.log1p(jnp.exp(-jnp.abs(x)))


def chunk_terms(step, age, bias_row, decay_row):
    raw = step + bias_row
    dt = softplus(raw)
    rate = -dt * decay_row
    rows = iota2((CHUNK, CHUNK), 0)
    cols = iota2((CHUNK, CHUNK), 1)
    lower = (cols <= rows).astype(F32)
    total = mm_exact(lower, rate)
    pos = iota2((CHUNK, 1), 0)
    first = pos - age
    bias = jnp.where((cols <= rows) & (cols >= first), 0.0, FAR)
    first_last = first[CHUNK - 1 :, :]
    enter = jnp.exp(total) * (first < 0).astype(F32)
    last = total[CHUNK - 1 :, :]
    leave = jnp.exp(last - total) * (pos >= first_last).astype(F32)
    through = jnp.exp(last) * (first_last < 0).astype(F32)
    return raw, dt, rate, total, bias, enter, leave, through


def to_order(refs, buf, shift, count):
    for k in range(count):
        buf[jnp.bitwise_xor(shift, k)] = refs[k][0]


def conv_sum(ext, age, weights, bias_row, rows):
    out = jnp.zeros((rows, ext.shape[1]), F32) + bias_row
    for j in range(4):
        part = ext[pl.ds(HALO - j, rows), :]
        if j:
            part = jnp.where(age >= j, part, 0.0)
        out = out + weights[3 - j : 4 - j, :] * part
    return out


def forward_kernel(shift_ref, *refs, count, cd, with_grad):
    mixed_refs, refs = refs[:count], refs[count:]
    if with_grad:
        grad_refs, refs = refs[:count], refs[count:]
    age_ref, pc_ref, ph_ref, refs = refs[0], refs[1], refs[2], refs[3:]
    gated_ref, pre_ref, ssd_ref, states_ref, refs = refs[0], refs[1], refs[2], refs[3], refs[4:]
    if with_grad:
        sums_ref, refs = refs[0], refs[1:]
    mixed_buf, gated_buf, ext, state, refs = refs[0], refs[1], refs[2], refs[3], refs[4:]
    if with_grad:
        grad_buf = refs[0]
    step_at = pl.program_id(0)
    shift = shift_ref[0]
    conv_ch = cd + 2 * STATE
    rows = mixed_buf.shape[0] * mixed_buf.shape[1]
    width = mixed_buf.shape[2]

    @pl.when(step_at == 0)
    def _():
        ext[0:HALO, :] = jnp.zeros((HALO, conv_ch), F32)
        state[...] = jnp.zeros_like(state)

    @pl.when(step_at > 0)
    def _():
        ext[0:HALO, :] = ext[rows : rows + HALO, :]

    to_order(mixed_refs, mixed_buf, shift, count)
    mixed = mixed_buf[...].reshape(rows, width)
    ext[HALO : HALO + rows, :] = mixed[:, cd : cd + conv_ch]
    age = age_ref[0][:rows, :]
    pre = conv_sum(ext, age, pc_ref[0:4, :], pc_ref[4:5, :], rows)
    pre_ref[0] = pre
    xbc = (pre * jax.nn.sigmoid(pre)).astype(BF)
    skip_row = pc_ref[5:6, :cd]
    gain_row = pc_ref[6:7, :cd]
    bias_row = ph_ref[0:1, :]
    decay_row = ph_ref[1:2, :]
    spread = head_spread(cd)
    low_half = iota2((CHUNK, LANES), 1) < HEAD_DIM
    outs = []
    for c in range(rows // CHUNK):
        at = slice(c * CHUNK, (c + 1) * CHUNK)
        raw, dt, rate, total, bias, enter, leave, through = chunk_terms(
            mixed[at, cd + conv_ch :], age[at], bias_row, decay_row
        )
        values = xbc[at, :cd]
        writers = xbc[at, cd : cd + STATE]
        readers = xbc[at, cd + STATE :]
        total_t = total.T
        dt_t = dt.T
        wide = mm_exact(
            jnp.concatenate([enter, leave * dt, jnp.broadcast_to(through, (8, LANES))], axis=0),
            spread,
        )
        scores = mm_bt(readers, writers)
        held = state[...]
        states_ref[0, c] = held.astype(BF)
        carried = mm(readers, held.astype(BF)) * wide[:CHUNK]
        values_f = values.astype(F32)
        pairs = []
        for pr in range(cd // LANES):
            mixing = []
            for h in (2 * pr, 2 * pr + 1):
                gap = total[:, h : h + 1] - total_t[h : h + 1, :] + bias
                mixing.append((jnp.exp(gap) * scores * dt_t[h : h + 1, :]).astype(BF))
            pair = values[:, pr * LANES : (pr + 1) * LANES]
            zero = jnp.zeros_like(pair)
            stacked = jnp.concatenate(
                [jnp.where(low_half, pair, zero), jnp.where(low_half, zero, pair)], axis=0
            )
            pairs.append(mm(jnp.concatenate(mixing, axis=1), stacked))
        ssd = jnp.concatenate(pairs, axis=1) + carried + skip_row * values_f
        state[...] = held * wide[2 * CHUNK : 2 * CHUNK + 1] + mm_at(
            writers, (wide[CHUNK : 2 * CHUNK] * values_f).astype(BF)
        )
        outs.append(ssd)
    ssd = jnp.concatenate(outs, axis=0)
    ssd_ref[0] = ssd
    gate = mixed[:, :cd]
    v = ssd * (gate * jax.nn.sigmoid(gate))
    squares = v * v
    partial_sums = squares[:, :LANES]
    for b in range(1, cd // LANES):
        partial_sums = partial_sums + squares[:, b * LANES : (b + 1) * LANES]
    weighted = v * gain_row
    gated_buf[:, :, :cd] = weighted.astype(BF).reshape(gated_buf.shape[0], gated_buf.shape[1], cd)
    if with_grad:
        to_order(grad_refs, grad_buf, shift, count)
        crossed = grad_buf[...].reshape(rows, cd) * weighted
        s1 = jnp.sum(partial_sums, axis=1, keepdims=True)
        s2 = jnp.sum(crossed, axis=1, keepdims=True)
        lane = iota2((rows, LANES), 1)
        sums_ref[0] = jnp.where(lane == 0, s1, jnp.where(lane == 1, s2, 0.0))
    else:
        gated_buf[:, :, cd:] = partial_sums.astype(BF).reshape(
            gated_buf.shape[0], gated_buf.shape[1], LANES
        )
    for k in range(count):
        gated_ref[k, 0] = gated_buf[jnp.bitwise_xor(shift, k)]


def backward_kernel(shift_ref, *refs, count, cd, own_scales):
    mixed_refs, grad_refs, refs = refs[:count], refs[count : 2 * count], refs[2 * count :]
    if own_scales:
        scale_ref, refs = refs[0], refs[1:]
    age_ref, pc_ref, ph_ref, pre_ref, ssd_ref, states_ref = refs[:6]
    out_ref, wide_sums, head_sums, mixed_buf, grad_buf, out_buf, ext, adjoint = refs[6:]
    step_at = pl.program_id(0)
    shift = shift_ref[0]
    conv_ch = cd + 2 * STATE
    q = mixed_buf.shape[1]
    rows = count * q
    width = mixed_buf.shape[2]

    @pl.when(step_at == 0)
    def _():
        ext[rows : rows + HALO, :] = jnp.zeros((HALO, conv_ch), F32)
        adjoint[...] = jnp.zeros_like(adjoint)
        wide_sums[...] = jnp.zeros_like(wide_sums)
        head_sums[...] = jnp.zeros_like(head_sums)

    @pl.when(step_at > 0)
    def _():
        ext[rows : rows + HALO, :] = ext[0:HALO, :]

    to_order(mixed_refs, mixed_buf, shift, count)
    to_order(grad_refs, grad_buf, shift, count)
    mixed = mixed_buf[...].reshape(rows, width)
    grad = grad_buf[...].reshape(rows, grad_buf.shape[2])
    age_ext = age_ref[0]
    age = age_ext[:rows, :]
    skip_row = pc_ref[5:6, :cd]
    gain_row = pc_ref[6:7, :cd]
    bias_row = ph_ref[0:1, :]
    decay_row = ph_ref[1:2, :]

    gate = mixed[:, :cd]
    ssd = ssd_ref[0]
    sg = jax.nn.sigmoid(gate)
    sl = gate * sg
    v = ssd * sl
    if own_scales:
        scaled = grad[:, :cd] * scale_ref[0][:, 0:1]
        mean_term = scale_ref[0][:, 1:2]
    else:
        scaled = grad[:, :cd]
        mean_term = grad[:, cd : cd + 1] + grad[:, cd + 1 : cd + 2]
    v_grad = scaled * gain_row - mean_term * v
    wide_sums[6:7, :cd] += jnp.sum(scaled * v, axis=0, keepdims=True)
    d_ssd = v_grad * sl
    d_gate = v_grad * ssd * (sg * (1.0 + gate * (1.0 - sg)))
    out_buf[:, :, :cd] = d_gate.astype(BF).reshape(count, q, cd)

    pre = pre_ref[0]
    sp = jax.nn.sigmoid(pre)
    xbc = (pre * sp).astype(BF)
    d_silu = sp * (1.0 + pre * (1.0 - sp))
    spread = head_spread(cd)
    gather = head_gather(cd)
    low_half = iota2((CHUNK, LANES), 1) < HEAD_DIM
    tri_rows = iota2((CHUNK, CHUNK), 0)
    tri_cols = iota2((CHUNK, CHUNK), 1)
    from_here = (tri_cols >= tri_rows).astype(F32)
    before = (tri_cols < tri_rows).astype(F32)
    heads = cd // HEAD_DIM
    pick = (iota2((heads * CHUNK, LANES), 0) // CHUNK == iota2((heads * CHUNK, LANES), 1)).astype(
        BF
    )

    def per_head(x):
        high = x.astype(BF)
        return mm(high, gather) + mm((x - high.astype(F32)).astype(BF), gather)

    for c in reversed(range(rows // CHUNK)):
        at = slice(c * CHUNK, (c + 1) * CHUNK)
        raw, dt, rate, total, bias, enter, leave, through = chunk_terms(
            mixed[at, cd + conv_ch :], age[at], bias_row, decay_row
        )
        values = xbc[at, :cd]
        writers = xbc[at, cd : cd + STATE]
        readers = xbc[at, cd + STATE :]
        values_f = values.astype(F32)
        dy = d_ssd[at]
        wide_sums[5:6, :cd] += jnp.sum(values_f * dy, axis=0, keepdims=True)
        total_t = total.T
        dt_t = dt.T
        wide = mm_exact(
            jnp.concatenate([enter, leave, dt, jnp.broadcast_to(through, (8, LANES))], axis=0),
            spread,
        )
        enter_w = wide[:CHUNK]
        leave_w = wide[CHUNK : 2 * CHUNK]
        dt_w = wide[2 * CHUNK : 3 * CHUNK]
        through_w = wide[3 * CHUNK : 3 * CHUNK + 1]
        held = states_ref[0, c]
        adj = adjoint[...]
        adj_b = adj.astype(BF)
        scores = mm_bt(readers, writers)
        entered = enter_w * dy
        entered_b = entered.astype(BF)
        row_enter = per_head(entered * mm(readers, held))
        d_readers = mm_bt(entered_b, held)
        from_state = leave_w * mm(writers, adj_b)
        exits = per_head(values_f * from_state * dt_w)
        d_writers = mm_bt((leave_w * dt_w * values_f).astype(BF), adj_b)
        through_sum = jnp.sum(adj * held.astype(F32), axis=0, keepdims=True) * through_w
        passing = per_head(jnp.broadcast_to(through_sum, (8, cd)))[0:1]
        adjoint[...] = adj * through_w + mm_at(readers, entered_b)
        d_scores = jnp.zeros((CHUNK, CHUNK), F32)
        pulls = []
        kernels = []
        for pr in range(cd // LANES):
            dy_pair = dy[:, pr * LANES : (pr + 1) * LANES].astype(BF)
            zero = jnp.zeros_like(dy_pair)
            stacked = jnp.concatenate(
                [jnp.where(low_half, dy_pair, zero), jnp.where(low_half, zero, dy_pair)], axis=0
            )
            d_mix = mm_bt(stacked, values[:, pr * LANES : (pr + 1) * LANES])
            mixing = []
            for i, h in enumerate((2 * pr, 2 * pr + 1)):
                gap = total[:, h : h + 1] - total_t[h : h + 1, :] + bias
                decays = jnp.exp(gap)
                mixing.append((decays * scores).astype(BF))
                pull = d_mix[i * CHUNK : (i + 1) * CHUNK] * dt_t[h : h + 1, :] * decays
                d_scores = d_scores + pull
                kernels.append((pull * scores).astype(BF))
            pulls.append(mm_at(jnp.concatenate(mixing, axis=0), stacked))
        d_scaled = jnp.concatenate(pulls, axis=1) + from_state
        row_sums = mm(jnp.concatenate(kernels, axis=1), pick)
        col_sums = mm_at(jnp.concatenate(kernels, axis=0), pick)
        d_rate = (
            mm_exact(from_here, row_sums - col_sums + row_enter)
            + mm_exact(before, exits)
            + passing
        )
        d_dt = per_head(values_f * d_scaled)
        d_raw = (d_dt - d_rate * decay_row) * jax.nn.sigmoid(raw)
        head_sums[0:1, :] += jnp.sum(d_raw, axis=0, keepdims=True)
        head_sums[1:2, :] += jnp.sum(d_rate * rate, axis=0, keepdims=True)
        d_scores_b = d_scores.astype(BF)
        d_readers = d_readers + mm(d_scores_b, writers)
        d_writers = d_writers + mm_at(d_scores_b, readers)
        d_values = dt_w * d_scaled + skip_row * dy
        ext[at, :] = jnp.concatenate([d_values, d_writers, d_readers], axis=1) * d_silu[at]
        per = CHUNK // q
        out_buf[c * per : (c + 1) * per, :, cd + conv_ch :] = d_raw.astype(BF).reshape(per, q, LANES)
    conv_in = mixed[:, cd : cd + conv_ch]
    d_conv = jnp.zeros((rows, conv_ch), F32)
    for j in range(4):
        part = ext[pl.ds(j, rows), :]
        if j:
            part = jnp.where(age_ext[j : j + rows, :] >= j, part, 0.0)
        else:
            wide_sums[4:5, :] += jnp.sum(part, axis=0, keepdims=True)
        d_conv = d_conv + pc_ref[3 - j : 4 - j, :] * part
        wide_sums[3 - j : 4 - j, :] += jnp.sum(part * conv_in, axis=0, keepdims=True)
    out_buf[:, :, cd : cd + conv_ch] = d_conv.astype(BF).reshape(count, q, conv_ch)
    for k in range(count):
        out_ref[k, 0] = out_buf[jnp.bitwise_xor(shift, k)]


def whole(shape):
    return pl.BlockSpec(shape, lambda *_: (0,) * len(shape))


def mixer_forward(shift, mixed, grads, age, pc, ph):
    count = len(mixed)
    blocks, q, width = mixed[0].shape
    conv_ch = pc.shape[1]
    cd = conv_ch - 2 * STATE
    rows = count * q
    with_grad = grads is not None
    out_width = cd if with_grad else cd + LANES
    shard = pl.BlockSpec((1, q, width), lambda i, s: (i, 0, 0))
    in_specs = [shard] * count
    args = list(mixed)
    if with_grad:
        in_specs += [pl.BlockSpec((1, q, cd), lambda i, s: (i, 0, 0))] * count
        args += list(grads)
    in_specs += [
        pl.BlockSpec((1, rows + HALO, 1), lambda i, s: (i, 0, 0)),
        whole(pc.shape),
        whole(ph.shape),
    ]
    args += [age, pc, ph]
    chunks = rows // CHUNK
    out_shape = [
        jax.ShapeDtypeStruct((count, blocks, q, out_width), BF),
        jax.ShapeDtypeStruct((blocks, rows, conv_ch), F32),
        jax.ShapeDtypeStruct((blocks, rows, cd), F32),
        jax.ShapeDtypeStruct((blocks, chunks, STATE, cd), BF),
    ]
    out_specs = [
        pl.BlockSpec((count, 1, q, out_width), lambda i, s: (0, i, 0, 0)),
        pl.BlockSpec((1, rows, conv_ch), lambda i, s: (i, 0, 0)),
        pl.BlockSpec((1, rows, cd), lambda i, s: (i, 0, 0)),
        pl.BlockSpec((1, chunks, STATE, cd), lambda i, s: (i, 0, 0, 0)),
    ]
    scratch = [
        pltpu.VMEM((count, q, width), F32),
        pltpu.VMEM((count, q, out_width), BF),
        pltpu.VMEM((rows + HALO, conv_ch), F32),
        pltpu.VMEM((STATE, cd), F32),
    ]
    if with_grad:
        out_shape.append(jax.ShapeDtypeStruct((blocks, rows, LANES), F32))
        out_specs.append(pl.BlockSpec((1, rows, LANES), lambda i, s: (i, 0, 0)))
        scratch.append(pltpu.VMEM((count, q, cd), F32))
    return pl.pallas_call(
        partial(forward_kernel, count=count, cd=cd, with_grad=with_grad),
        out_shape=out_shape,
        grid_spec=pltpu.PrefetchScalarGridSpec(
            num_scalar_prefetch=1,
            grid=(blocks,),
            in_specs=in_specs,
            out_specs=out_specs,
            scratch_shapes=scratch,
        ),
        compiler_params=pltpu.CompilerParams(vmem_limit_bytes=48 * 2**20),
        cost_estimate=pl.CostEstimate(
            flops=10**10, bytes_accessed=3 * 10**7, transcendentals=10**6
        ),
    )(shift, *args)


def mixer_backward(shift, mixed, grads, scales, age, pc, ph, pre, ssd, states):
    count = len(mixed)
    blocks, q, width = mixed[0].shape
    conv_ch = pc.shape[1]
    cd = conv_ch - 2 * STATE
    rows = count * q
    chunks = rows // CHUNK
    top = blocks - 1
    grad_width = grads[0].shape[2]
    in_specs = [pl.BlockSpec((1, q, width), lambda i, s: (top - i, 0, 0))] * count
    in_specs += [pl.BlockSpec((1, q, grad_width), lambda i, s: (top - i, 0, 0))] * count
    args = list(mixed) + list(grads)
    if scales is not None:
        in_specs.append(pl.BlockSpec((1, rows, 2), lambda i, s: (top - i, 0, 0)))
        args.append(scales)
    in_specs += [
        pl.BlockSpec((1, rows + HALO, 1), lambda i, s: (top - i, 0, 0)),
        whole(pc.shape),
        whole(ph.shape),
        pl.BlockSpec((1, rows, conv_ch), lambda i, s: (top - i, 0, 0)),
        pl.BlockSpec((1, rows, cd), lambda i, s: (top - i, 0, 0)),
        pl.BlockSpec((1, chunks, STATE, cd), lambda i, s: (top - i, 0, 0, 0)),
    ]
    args += [age, pc, ph, pre, ssd, states]
    return pl.pallas_call(
        partial(backward_kernel, count=count, cd=cd, own_scales=scales is not None),
        out_shape=[
            jax.ShapeDtypeStruct((count, blocks, q, width), BF),
            jax.ShapeDtypeStruct((8, conv_ch), F32),
            jax.ShapeDtypeStruct((8, LANES), F32),
        ],
        grid_spec=pltpu.PrefetchScalarGridSpec(
            num_scalar_prefetch=1,
            grid=(blocks,),
            in_specs=in_specs,
            out_specs=[
                pl.BlockSpec((count, 1, q, width), lambda i, s: (0, top - i, 0, 0)),
                whole((8, conv_ch)),
                whole((8, LANES)),
            ],
            scratch_shapes=[
                pltpu.VMEM((count, q, width), F32),
                pltpu.VMEM((count, q, grad_width), F32),
                pltpu.VMEM((count, q, width), BF),
                pltpu.VMEM((rows + HALO, conv_ch), F32),
                pltpu.VMEM((STATE, cd), F32),
            ],
        ),
        compiler_params=pltpu.CompilerParams(vmem_limit_bytes=48 * 2**20),
        cost_estimate=pl.CostEstimate(
            flops=2 * 10**10, bytes_accessed=5 * 10**7, transcendentals=2 * 10**6
        ),
    )(shift, *args)


def swap(value, axis, k, size):
    return lax.ppermute(value, axis, [(i, i ^ k) for i in range(size)])


def pick(value, index):
    return lax.dynamic_index_in_dim(value, index, 0, keepdims=False)


def exchange(parts, axis, size):
    mine = lax.axis_index(axis)
    return [pick(parts, mine)] + [
        swap(pick(parts, mine ^ k), axis, k, size) for k in range(1, size)
    ]


def in_order(relative, mine):
    stacked = jnp.stack(relative)
    return jnp.stack([pick(stacked, mine ^ j) for j in range(len(relative))])


def gather_rows(shard, n):
    if n != 4:
        everything = lax.all_gather(shard, "dp")
        mine = lax.axis_index("dp")
        return [pick(everything, mine ^ k) for k in range(n)]
    half = shard.shape[0] // 2
    first = swap(shard, "dp", 1, n)
    second = swap(shard, "dp", 2, n)
    low = swap(first[:half], "dp", 2, n)
    high = swap(second[half:], "dp", 1, n)
    return [shard, first, second, jnp.concatenate([low, high], axis=0)]


def reduce_rows(parts, n):
    if n != 4:
        mine = lax.axis_index("dp")
        ordered = jnp.stack([pick(parts, mine ^ j) for j in range(n)])
        return lax.psum_scatter(ordered, "dp", scatter_dimension=0, tiled=False).astype(F32)
    half = parts.shape[1] // 2
    a, b = parts[:, :half], parts[:, half:]
    got_a = swap(jnp.stack([a[1], a[3]]), "dp", 1, n)
    got_b = swap(jnp.stack([b[2], b[3]]), "dp", 2, n)
    on_a = (a[2].astype(F32) + got_a[1].astype(F32)).astype(BF)
    on_b = (b[1].astype(F32) + got_b[1].astype(F32)).astype(BF)
    last_a = swap(on_a, "dp", 2, n)
    last_b = swap(on_b, "dp", 1, n)
    sum_a = a[0].astype(F32) + got_a[0].astype(F32) + last_a.astype(F32)
    sum_b = b[0].astype(F32) + got_b[0].astype(F32) + last_b.astype(F32)
    return jnp.concatenate([sum_a, sum_b], axis=0)


def tokens_in(block, n, z_count):
    core = lax.axis_index("core")
    keep = pick(block, core)
    other = lax.ppermute(pick(block, 1 - core), "core", [(0, 1), (1, 0)])
    first = jnp.where(core == 0, keep, other)
    second = jnp.where(core == 0, other, keep)
    both = jnp.concatenate([first, second], axis=0)
    q = both.shape[0] // n
    by_group = exchange(both.reshape(n, q, -1), "dp", n)
    ordered = in_order(by_group, lax.axis_index("dp"))
    by_chunk = exchange(ordered, "z", z_count)
    return in_order(by_chunk, lax.axis_index("z"))


def tokens_out(own, n, z_count):
    core = lax.axis_index("core")
    q = own.shape[1]
    by_group = in_order(exchange(own, "z", z_count), lax.axis_index("z"))
    by_part = in_order(exchange(by_group, "dp", n), lax.axis_index("dp"))
    both = by_part.reshape(2, n * q // 2, -1)
    keep = pick(both, core)
    other = lax.ppermute(pick(both, 1 - core), "core", [(0, 1), (1, 0)])
    return jnp.stack([jnp.where(core == 0, keep, other), jnp.where(core == 0, other, keep)])


def on_device(
    hidden_in,
    doc_lengths,
    norm_gain,
    input_proj,
    step_proj,
    conv_weight,
    conv_bias,
    step_bias,
    decay_log,
    skip_gain,
    gate_gain,
    output_proj,
    cotangent,
    *,
    n,
    z_count,
):
    layers = norm_gain.shape[0]
    owners = 2 * z_count
    d_rows = norm_gain.shape[1]
    width_d = d_rows * owners
    heads_f = step_bias.shape[1]
    heads = heads_f * owners
    hd = heads // n
    cd = hd * HEAD_DIM
    inner = heads * HEAD_DIM
    conv_f = conv_bias.shape[1]
    conv_ch = cd + 2 * STATE
    gate_f = gate_gain.shape[1]
    out_rows = output_proj.shape[1]
    width_in = cd + conv_ch + LANES
    step_at = cd + conv_ch
    d = lax.axis_index("dp")
    z = lax.axis_index("z")
    core = lax.axis_index("core")
    shift = (d if n else d).astype(jnp.int32).reshape(1)

    small_len = 5 * conv_f + gate_f + 3 * heads_f
    small_cols = -(-small_len // d_rows)

    def small_pack(cw, cb, gg, sb, dl, sk):
        flat = jnp.concatenate([cw.reshape(-1), cb, gg, sb, dl, sk])
        return jnp.pad(flat, (0, small_cols * d_rows - small_len)).reshape(d_rows, small_cols)

    def small_split(flat):
        sizes = (4 * conv_f, conv_f, gate_f, heads_f, heads_f, heads_f)
        parts, at = [], 0
        for size in sizes:
            parts.append(flat[..., at : at + size])
            at += size
        return parts

    def weights_in(layer):
        block = input_proj[layer]
        pieces = jnp.concatenate(
            [
                lax.dynamic_slice_in_dim(block, d * cd, cd, 1),
                lax.dynamic_slice_in_dim(block, inner + d * cd, cd, 1),
                block[:, 2 * inner :],
                lax.dynamic_slice_in_dim(step_proj[layer], d * hd, hd, 0).T,
            ],
            axis=1,
        )
        pieces = (pieces.astype(F32) * norm_gain[layer].astype(F32)[:, None]).astype(BF)
        small = small_pack(
            conv_weight[layer],
            conv_bias[layer],
            gate_gain[layer],
            step_bias[layer],
            decay_log[layer],
            skip_gain[layer],
        )
        rest = LANES - hd - small_cols
        shard = jnp.concatenate([pieces, small, jnp.zeros((d_rows, rest), BF)], axis=1)
        full = lax.all_gather(shard, PLANE, tiled=True)
        small_all = full[:, step_at + hd : step_at + hd + small_cols].astype(F32)
        cw, cb, gg, sb, dl, sk = small_split(small_all.reshape(owners, small_cols * d_rows))
        conv = jnp.concatenate([cw, cb], axis=1).reshape(owners, 5, conv_f)
        conv = conv.transpose(1, 0, 2).reshape(5, owners * conv_f)
        conv = jnp.concatenate(
            [lax.dynamic_slice_in_dim(conv, d * cd, cd, 1), conv[:, inner:]], axis=1
        )
        gain = lax.dynamic_slice_in_dim(gg.reshape(-1), d * cd, cd, 0)
        sk = lax.dynamic_slice_in_dim(sk.reshape(-1), d * hd, hd, 0)
        sb = lax.dynamic_slice_in_dim(sb.reshape(-1), d * hd, hd, 0)
        dl = lax.dynamic_slice_in_dim(dl.reshape(-1), d * hd, hd, 0)
        skip = jnp.broadcast_to(sk[:, None], (hd, HEAD_DIM)).reshape(-1)
        wide = jnp.pad(jnp.stack([skip, gain]), ((0, 1), (0, 2 * STATE)))
        pc = jnp.concatenate([conv, wide], axis=0)
        ph = jnp.pad(jnp.stack([sb, jnp.exp(dl)]), ((0, 6), (0, LANES - hd)))
        keep = (iota2((1, width_in), 1) < step_at + hd).astype(BF)
        return full * keep, pc, ph

    out_cols = width_d // n

    def weights_out(layer):
        mine = lax.dynamic_slice_in_dim(output_proj[layer], d * out_cols, out_cols, 1)
        column = lax.all_gather(mine, PLANE, tiled=True)
        parts = exchange(column.reshape(n, cd, out_cols), "dp", n)
        full = jnp.zeros((cd, width_d), BF)
        for k in range(n):
            full = lax.dynamic_update_slice(full, parts[k], (0, (d ^ k) * out_cols))
        return full

    both = lax.ppermute(
        doc_lengths,
        ("dp", "z"),
        [(i * z_count + j, j * z_count + i) for i in range(n) for j in range(z_count)],
    )
    ends = jnp.cumsum(pick(both, core))
    tok = hidden_in.shape[1]
    block_rows = 2 * tok
    row_len = block_rows * z_count
    q = block_rows // n
    positions = jnp.arange(row_len, dtype=jnp.int32)
    begin = jnp.max(jnp.where(ends[None, :] <= positions[:, None], ends[None, :], 0), axis=1)
    age = (positions - begin).reshape(z_count, block_rows)
    after = jnp.concatenate([age[1:, :HALO], jnp.zeros((1, HALO), jnp.int32)], axis=0)
    age = jnp.concatenate([age, after], axis=1)[:, :, None]

    w_in = [None] * layers
    w_out = [None] * layers
    pcs = [None] * layers
    phs = [None] * layers
    for layer in range(layers):
        w_in[layer], pcs[layer], phs[layer] = weights_in(layer)
        w_out[layer] = weights_out(layer)

    def extended(weight):
        eye = jnp.eye(LANES, dtype=BF)
        return jnp.concatenate(
            [
                jnp.pad(weight, ((0, 0), (0, LANES))),
                jnp.pad(eye, ((0, 0), (width_d, 0))),
            ],
            axis=0,
        )

    def normalize(resid):
        inv = lax.rsqrt(jnp.mean(resid * resid, axis=-1, keepdims=True) + EPSILON)
        return inv, resid * inv

    def flat(x):
        return x.reshape(-1, x.shape[-1])

    resid = tokens_in(hidden_in, n, z_count).astype(F32)
    upstream = tokens_in(cotangent, n, z_count)
    upstream_all = gather_rows(upstream, n)

    kept = [None] * layers
    last = layers - 1
    for layer in range(layers):
        inv, u = normalize(resid)
        unit_all = gather_rows(u.astype(BF), n)
        mixed = [
            mm(flat(part), w_in[layer]).reshape(z_count, q, width_in) for part in unit_all
        ]
        if layer < last:
            weight = extended(w_out[layer])
            gated, pre, ssd, states = mixer_forward(
                shift, mixed, None, age, pcs[layer], phs[layer]
            )
            sent = mm(flat(gated), weight).astype(BF).reshape(n, z_count, q, width_d + LANES)
            got = reduce_rows(sent, n)
            squares = jnp.sum(got[..., width_d:], axis=-1, keepdims=True)
            ginv = lax.rsqrt(squares / inner + EPSILON)
            branch = got[..., :width_d] * ginv
            kept[layer] = (resid, inv, unit_all, mixed, gated, pre, ssd, states, weight, ginv, branch)
            resid = resid + branch
        else:
            weight = w_out[layer]
            gg = [mm_bt(flat(part), weight).reshape(z_count, q, cd) for part in upstream_all]
            gated, pre, ssd, states, sums = mixer_forward(
                shift, mixed, gg, age, pcs[layer], phs[layer]
            )
            totals = sums[:, :, :2].transpose(2, 0, 1).reshape(2, row_len // LANES, LANES)
            bit = 1
            while bit < n:
                totals = totals + swap(totals, "dp", bit, n)
                bit *= 2
            totals = totals.reshape(2, z_count, block_rows)
            ginv = lax.rsqrt(totals[0] / inner + EPSILON)
            scales = jnp.stack([ginv, ginv * ginv * ginv * totals[1] / inner], axis=-1)
            sent = mm(flat(gated), weight).astype(BF).reshape(n, z_count, q, width_d)
            own = lax.dynamic_index_in_dim(
                ginv.reshape(z_count, n, q), d, 1, keepdims=False
            )[..., None]
            hidden_out = (resid + reduce_rows(sent, n) * own).astype(BF)
            kept[layer] = (resid, inv, unit_all, mixed, gated, pre, ssd, states, weight, ginv, gg)
    hidden_out = tokens_out(hidden_out, n, z_count)

    back = upstream.astype(F32)
    results = [None] * layers
    for layer in reversed(range(layers)):
        resid, inv, unit_all, mixed, gated, pre, ssd, states, weight, ginv, extra = kept[layer]
        if layer == last:
            g_all = upstream_all
            gg = extra
            scale = ginv.reshape(z_count, n, q)
            scale = in_order([lax.dynamic_index_in_dim(scale, d ^ k, 1, False) for k in range(n)], 0)
            gated = (gated.astype(F32) * scale[..., None]).astype(BF)
            use = scales
        else:
            low = back.astype(BF).astype(F32)
            m = jnp.sum(low * extra, axis=-1, keepdims=True) / inner
            kappa = ginv * ginv * m
            high = kappa.astype(BF)
            rest = (kappa - high.astype(F32)).astype(BF)
            payload = jnp.concatenate(
                [(low * ginv).astype(BF), high, rest, jnp.zeros((z_count, q, LANES - 2), BF)],
                axis=-1,
            )
            g_all = gather_rows(payload, n)
            gg = [mm_bt(flat(part), weight).reshape(z_count, q, cd + LANES) for part in g_all]
            use = None
        d_mixed, wide_sums, head_sums = mixer_backward(
            shift, mixed, gg, use, age, pcs[layer], phs[layer], pre, ssd, states
        )
        sent = mm_bt(flat(d_mixed), w_in[layer]).astype(BF).reshape(n, z_count, q, width_d)
        normed_grad = reduce_rows(sent, n)
        u = resid * inv
        back = back + inv * (
            normed_grad - u * jnp.mean(normed_grad * u, axis=-1, keepdims=True)
        )
        g_cat = flat(jnp.stack(g_all))
        d_out = mm_at(flat(gated), g_cat)[:cd, :width_d].astype(BF)
        by_column = jnp.stack([d_out[:, j * out_cols : (j + 1) * out_cols] for j in range(n)])
        rows_all = in_order(exchange(by_column, "dp", n), d).reshape(n * cd, out_cols)
        own_out = lax.psum_scatter(rows_all, PLANE, scatter_dimension=0, tiled=True)
        out_grad = lax.all_gather(own_out, "dp", axis=1, tiled=True).astype(F32)

        d_in = mm_at(flat(jnp.stack(unit_all)), flat(d_mixed)).astype(BF)
        conv_full = jnp.concatenate([jnp.zeros((5, inner), F32), wide_sums[:5, cd:]], axis=1)
        conv_full = lax.dynamic_update_slice(conv_full, wide_sums[:5, :cd], (0, d * cd))
        conv_full = conv_full.reshape(5, owners, conv_f).transpose(1, 0, 2).reshape(owners, -1)
        gain_full = lax.dynamic_update_slice(jnp.zeros((inner,), F32), wide_sums[6, :cd], (d * cd,))
        skip_sum = jnp.sum(wide_sums[5, :cd].reshape(hd, HEAD_DIM), axis=1)
        head_full = lax.dynamic_update_slice(
            jnp.zeros((3, heads), F32),
            jnp.stack([head_sums[0, :hd], head_sums[1, :hd], skip_sum]),
            (0, d * hd),
        )
        head_full = head_full.reshape(3, owners, heads_f).transpose(1, 0, 2).reshape(owners, -1)
        small = jnp.concatenate([conv_full, gain_full.reshape(owners, gate_f), head_full], axis=1)
        small = jnp.pad(small, ((0, 0), (0, small_cols * d_rows - small_len)))
        small = small.reshape(owners * d_rows, small_cols).astype(BF)
        d_in = lax.dynamic_update_slice(d_in, small, (0, step_at + hd))
        own_in = lax.psum_scatter(d_in, PLANE, scatter_dimension=0, tiled=True)
        all_in = lax.all_gather(own_in, "dp").astype(F32)
        small = jnp.sum(all_in[:, :, step_at + hd : step_at + hd + small_cols], axis=0)
        small = small_split(small.reshape(-1)[:small_len])
        unit_grad = jnp.concatenate(
            [all_in[j, :, :cd] for j in range(n)]
            + [all_in[j, :, cd : 2 * cd] for j in range(n)]
            + [jnp.sum(all_in[:, :, 2 * cd : step_at], axis=0)],
            axis=1,
        )
        step_unit = jnp.concatenate(
            [all_in[j, :, step_at : step_at + hd] for j in range(n)], axis=1
        )
        gain = norm_gain[layer].astype(F32)
        norm_grad = jnp.sum(unit_grad * input_proj[layer].astype(F32), axis=1) + jnp.sum(
            step_unit.T * step_proj[layer].astype(F32), axis=0
        )
        results[layer] = (
            norm_grad,
            unit_grad * gain[:, None],
            step_unit.T * gain[None, :],
            small[0].reshape(4, conv_f),
            small[1],
            small[3],
            small[4],
            small[5],
            small[2],
            out_grad,
        )
    hidden_grad = tokens_out(back.astype(BF), n, z_count).astype(F32)
    stacked = tuple(
        jnp.stack([results[layer][member] for layer in range(layers)]) for member in range(10)
    )
    return (hidden_out, hidden_grad) + stacked


def solution(mesh):
    n = mesh.shape["dp"]
    z_count = mesh.shape["fsdp"] // 2
    assert n == z_count
    split = Mesh(mesh.devices.reshape(n, z_count, 2), ("dp", "z", "core"))
    fsdp = PLANE
    tokens = P("dp", fsdp, None)
    last = P(None, fsdp)
    weights = (
        last,
        P(None, fsdp, None),
        P(None, None, fsdp),
        P(None, None, fsdp),
        last,
        last,
        last,
        last,
        last,
        P(None, fsdp, None),
    )
    return jax.shard_map(
        partial(on_device, n=n, z_count=z_count),
        mesh=split,
        in_specs=(tokens, P("dp", None)) + weights + (tokens,),
        out_specs=(tokens, tokens) + weights,
        check_vma=False,
    )
```

```python
from functools import partial

import jax
import jax.numpy as jnp
from jax import lax
from jax.experimental import pallas as pl
from jax.experimental.pallas import tpu as pltpu
from jax.sharding import Mesh
from jax.sharding import PartitionSpec as P

BF = jnp.bfloat16
F32 = jnp.float32
HIGHEST = lax.Precision.HIGHEST
EPSILON = 1e-05
HEAD_DIM = 64
STATE = 128
LANES = 128
CHUNK = 128
HALO = 8
FAR = -1e30
PLANE = ("z", "core")


def mm(a, b):
    return lax.dot_general(a, b, (((1,), (0,)), ((), ())), preferred_element_type=F32)


def mm_bt(a, b):
    return lax.dot_general(a, b, (((1,), (1,)), ((), ())), preferred_element_type=F32)


def mm_at(a, b):
    return lax.dot_general(a, b, (((0,), (0,)), ((), ())), preferred_element_type=F32)


def halves(x, count):
    out = []
    for _ in range(count):
        part = x.astype(BF)
        out.append(part)
        x = x - part.astype(F32)
    return out


def mm_fine(a, b, count):
    return sum(mm(part, b) for part in halves(a, count))


def mm_fine_right(a, b, count):
    return sum(mm(a, part) for part in halves(b, count))


def iota2(shape, dim):
    return lax.broadcasted_iota(jnp.int32, shape, dim)


def head_spread(width):
    return (iota2((LANES, width), 1) // HEAD_DIM == iota2((LANES, width), 0)).astype(BF)


def head_gather(width):
    return (iota2((width, LANES), 0) // HEAD_DIM == iota2((width, LANES), 1)).astype(BF)


def softplus(x):
    return jnp.maximum(x, 0.0) + jnp.log1p(jnp.exp(-jnp.abs(x)))


def chunk_terms(step, age, bias_row, decay_row):
    raw = step + bias_row
    dt = softplus(raw)
    rate = -dt * decay_row
    rows = iota2((CHUNK, CHUNK), 0)
    cols = iota2((CHUNK, CHUNK), 1)
    lower = (cols <= rows).astype(BF)
    total = mm_fine_right(lower, rate, 3)
    pos = iota2((CHUNK, 1), 0)
    first = pos - age
    bias = jnp.where((cols <= rows) & (cols >= first), 0.0, FAR)
    first_last = first[CHUNK - 1 :, :]
    enter = jnp.exp(total) * (first < 0).astype(F32)
    last = total[CHUNK - 1 :, :]
    leave = jnp.exp(last - total) * (pos >= first_last).astype(F32)
    through = jnp.exp(last) * (first_last < 0).astype(F32)
    return raw, dt, rate, total, bias, enter, leave, through


def shard_refs(refs, count):
    used = count + 1 if count == 4 else count
    return refs[:used], refs[used:]


def to_order(refs, buf, shift, count, at):
    for k in range(count):
        place = jnp.bitwise_xor(shift, k)
        if count == 4 and k == 3:
            low, high, blocks = refs[3], refs[4], at[1]

            @pl.when(at[0] < blocks // 2)
            def _():
                buf[place] = low[0]

            @pl.when(at[0] >= blocks // 2)
            def _():
                buf[place] = high[0]

        else:
            buf[place] = refs[k][0]


def shard_specs(count, blocks, q, width, place):
    one = pl.BlockSpec((1, q, width), lambda i, s: (place(i, s), 0, 0))
    if count != 4:
        return [one] * count
    half = blocks // 2
    low = pl.BlockSpec((1, q, width), lambda i, s: (jnp.minimum(place(i, s), half - 1), 0, 0))
    high = pl.BlockSpec((1, q, width), lambda i, s: (jnp.maximum(place(i, s) - half, 0), 0, 0))
    return [one, one, one, low, high]


def conv_sum(ext, age, weights, bias_row, rows):
    out = jnp.zeros((rows, ext.shape[1]), F32) + bias_row
    for j in range(4):
        part = ext[pl.ds(HALO - j, rows), :]
        if j:
            part = jnp.where(age >= j, part, 0.0)
        out = out + weights[3 - j : 4 - j, :] * part
    return out


def forward_kernel(shift_ref, *refs, count, cd, ordered):
    unit_refs, refs = shard_refs(refs, count)
    weight_ref, age_ref, pc_ref, ph_ref, refs = *refs[:4], refs[4:]
    unit_ref, mixed_ref, gated_ref, pre_ref, ssd_ref, states_ref, sums_ref, refs = *refs[:7], refs[7:]
    unit_buf, gated_buf, ext, state, sums_buf = refs
    grid_at = pl.program_id(0)
    blocks = pl.num_programs(0)
    shift = shift_ref[0]
    conv_ch = cd + 2 * STATE
    q = unit_buf.shape[1]
    rows = count * q

    @pl.when(grid_at == 0)
    def _():
        ext[0:HALO, :] = jnp.zeros((HALO, conv_ch), F32)
        state[...] = jnp.zeros_like(state)

    @pl.when(grid_at > 0)
    def _():
        ext[0:HALO, :] = ext[rows : rows + HALO, :]

    to_order(unit_refs, unit_buf, shift, count, (jnp.bitwise_xor(grid_at, shift_ref[1]), blocks))
    unit = unit_buf[...].reshape(rows, unit_buf.shape[2])
    unit_ref[0] = unit
    mixed_ref[0] = mm(unit, weight_ref[...].reshape(-1, weight_ref.shape[2]))
    ext[HALO : HALO + rows, :] = mixed_ref[0, :, cd : cd + conv_ch]
    age = age_ref[0][:rows, :]
    pre = conv_sum(ext, age, pc_ref[0:4, :], pc_ref[4:5, :], rows)
    pre_ref[0] = pre
    xbc = (pre * jax.nn.sigmoid(pre)).astype(BF)
    skip_row = pc_ref[5:6, :cd]
    gain_row = pc_ref[6:7, :cd]
    bias_row = ph_ref[0:1, :]
    decay_row = ph_ref[1:2, :]
    spread = head_spread(cd)
    low_half = iota2((CHUNK, LANES), 1) < HEAD_DIM
    for c in range(rows // CHUNK):
        at = slice(c * CHUNK, (c + 1) * CHUNK)
        raw, dt, rate, total, bias, enter, leave, through = chunk_terms(
            mixed_ref[0, at, cd + conv_ch :], age[at], bias_row, decay_row
        )
        values = xbc[at, :cd]
        writers = xbc[at, cd : cd + STATE]
        readers = xbc[at, cd + STATE :]
        total_t = total.T
        dt_t = dt.T
        wide = mm_fine(
            jnp.concatenate([enter, leave * dt, jnp.broadcast_to(through, (8, LANES))], axis=0),
            spread,
            2,
        )
        scores = mm_bt(readers, writers)
        held = state[...]
        states_ref[0, c] = held.astype(BF)
        carried = mm(readers, held.astype(BF)) * wide[:CHUNK]
        values_f = values.astype(F32)
        pairs = []
        for pr in range(cd // LANES):
            mixing = []
            for h in (2 * pr, 2 * pr + 1):
                gap = total[:, h : h + 1] - total_t[h : h + 1, :] + bias
                mixing.append((jnp.exp(gap) * scores * dt_t[h : h + 1, :]).astype(BF))
            pair = values[:, pr * LANES : (pr + 1) * LANES]
            zero = jnp.zeros_like(pair)
            stacked = jnp.concatenate(
                [jnp.where(low_half, pair, zero), jnp.where(low_half, zero, pair)], axis=0
            )
            pairs.append(mm(jnp.concatenate(mixing, axis=1), stacked))
        ssd = jnp.concatenate(pairs, axis=1) + carried + skip_row * values_f
        ssd_ref[0, at, :] = ssd
        state[...] = held * wide[2 * CHUNK : 2 * CHUNK + 1] + mm_at(
            writers, (wide[CHUNK : 2 * CHUNK] * values_f).astype(BF)
        )
    ssd = ssd_ref[0]
    gate = mixed_ref[0, :, :cd]
    v = ssd * (gate * jax.nn.sigmoid(gate))
    squares = v * v
    partial_sums = squares[:, :LANES]
    for b in range(1, cd // LANES):
        partial_sums = partial_sums + squares[:, b * LANES : (b + 1) * LANES]
    weighted = v * gain_row
    gated = weighted.astype(BF).reshape(count, q, cd)
    sums = partial_sums.astype(BF).reshape(count, q, LANES)
    if ordered:
        gated_ref[:, 0] = gated
        sums_ref[:, 0] = sums
        return
    gated_buf[...] = gated
    sums_buf[...] = sums
    for k in range(count):
        gated_ref[k, 0] = gated_buf[jnp.bitwise_xor(shift, k)]
        sums_ref[k, 0] = sums_buf[jnp.bitwise_xor(shift, k)]


def backward_kernel(shift_ref, *refs, count, cd, own_scales):
    shift = shift_ref[0]
    grid_at = pl.program_id(0)
    blocks = pl.num_programs(0)
    if own_scales:
        grad_ref, scale_ref, refs = refs[0], refs[1], refs[2:]
    else:
        grad_refs, refs = shard_refs(refs, count)
        weight_out_ref, refs = refs[0], refs[1:]
    weight_ref, mixed_ref, age_ref, pc_ref, ph_ref, pre_ref, ssd_ref, states_ref = refs[:8]
    mixed_grad_ref, unit_grad_ref, wide_sums, head_sums = refs[8:12]
    out_buf, ext, adjoint = refs[12:15]
    conv_ch = cd + 2 * STATE
    rows = mixed_ref.shape[1]
    q = rows // count

    @pl.when(grid_at == 0)
    def _():
        ext[rows : rows + HALO, :] = jnp.zeros((HALO, conv_ch), F32)
        adjoint[...] = jnp.zeros_like(adjoint)
        wide_sums[...] = jnp.zeros_like(wide_sums)
        head_sums[...] = jnp.zeros_like(head_sums)

    @pl.when(grid_at > 0)
    def _():
        ext[rows : rows + HALO, :] = ext[0:HALO, :]

    age_ext = age_ref[0]
    age = age_ext[:rows, :]
    skip_row = pc_ref[5:6, :cd]
    gain_row = pc_ref[6:7, :cd]
    bias_row = ph_ref[0:1, :]
    decay_row = ph_ref[1:2, :]

    if own_scales:
        extra = scale_ref[:, 0].reshape(rows, 2)
        scaled = grad_ref[:, 0].reshape(rows, cd) * extra[:, 0:1]
        mean_term = extra[:, 1:2]
    else:
        grad_buf = refs[15]
        at = jnp.bitwise_xor(blocks - 1 - grid_at, shift_ref[1])
        to_order(grad_refs, grad_buf, shift, count, (at, blocks))
        grad = grad_buf[...].reshape(rows, grad_buf.shape[2])
        model = weight_out_ref.shape[1]
        scaled = mm_bt(grad[:, :model], weight_out_ref[...])
        extra = grad[:, model:].astype(F32)
        mean_term = extra[:, 0:1] + extra[:, 1:2]
    gate = mixed_ref[0, :, :cd]
    ssd = ssd_ref[0]
    sg = jax.nn.sigmoid(gate)
    sl = gate * sg
    v = ssd * sl
    v_grad = scaled * gain_row - mean_term * v
    wide_sums[6:7, :cd] += jnp.sum(scaled * v, axis=0, keepdims=True)
    d_ssd = v_grad * sl
    d_gate = v_grad * ssd * (sg * (1.0 + gate * (1.0 - sg)))
    out_buf[:, :cd] = d_gate.astype(BF)

    pre = pre_ref[0]
    sp = jax.nn.sigmoid(pre)
    xbc = (pre * sp).astype(BF)
    d_silu = sp * (1.0 + pre * (1.0 - sp))
    spread = head_spread(cd)
    gather = head_gather(cd)
    low_half = iota2((CHUNK, LANES), 1) < HEAD_DIM
    tri_rows = iota2((CHUNK, CHUNK), 0)
    tri_cols = iota2((CHUNK, CHUNK), 1)
    from_here = (tri_cols >= tri_rows).astype(BF)
    before = (tri_cols < tri_rows).astype(BF)
    heads = cd // HEAD_DIM
    pick_shape = (heads * CHUNK, LANES)
    pick_head = (iota2(pick_shape, 0) // CHUNK == iota2(pick_shape, 1)).astype(BF)

    for c in reversed(range(rows // CHUNK)):
        at = slice(c * CHUNK, (c + 1) * CHUNK)
        raw, dt, rate, total, bias, enter, leave, through = chunk_terms(
            mixed_ref[0, at, cd + conv_ch :], age[at], bias_row, decay_row
        )
        values = xbc[at, :cd]
        writers = xbc[at, cd : cd + STATE]
        readers = xbc[at, cd + STATE :]
        values_f = values.astype(F32)
        dy = d_ssd[at]
        wide_sums[5:6, :cd] += jnp.sum(values_f * dy, axis=0, keepdims=True)
        total_t = total.T
        dt_t = dt.T
        wide = mm_fine(
            jnp.concatenate([enter, leave, dt, jnp.broadcast_to(through, (8, LANES))], axis=0),
            spread,
            2,
        )
        enter_w = wide[:CHUNK]
        leave_w = wide[CHUNK : 2 * CHUNK]
        dt_w = wide[2 * CHUNK : 3 * CHUNK]
        through_w = wide[3 * CHUNK : 3 * CHUNK + 1]
        held = states_ref[0, c]
        adj = adjoint[...]
        adj_b = adj.astype(BF)
        scores = mm_bt(readers, writers)
        entered = enter_w * dy
        entered_b = entered.astype(BF)
        row_enter = entered * mm(readers, held)
        d_readers = mm_bt(entered_b, held)
        from_state = leave_w * mm(writers, adj_b)
        exits = values_f * from_state * dt_w
        d_writers = mm_bt((leave_w * dt_w * values_f).astype(BF), adj_b)
        through_sum = jnp.sum(adj * held.astype(F32), axis=0, keepdims=True) * through_w
        adjoint[...] = adj * through_w + mm_at(readers, entered_b)
        d_scores = jnp.zeros((CHUNK, CHUNK), F32)
        pulls = []
        kernels = []
        for pr in range(cd // LANES):
            dy_pair = dy[:, pr * LANES : (pr + 1) * LANES].astype(BF)
            zero = jnp.zeros_like(dy_pair)
            stacked = jnp.concatenate(
                [jnp.where(low_half, dy_pair, zero), jnp.where(low_half, zero, dy_pair)], axis=0
            )
            d_mix = mm_bt(stacked, values[:, pr * LANES : (pr + 1) * LANES])
            mixing = []
            for i, h in enumerate((2 * pr, 2 * pr + 1)):
                gap = total[:, h : h + 1] - total_t[h : h + 1, :] + bias
                decays = jnp.exp(gap)
                mixing.append((decays * scores).astype(BF))
                pull = d_mix[i * CHUNK : (i + 1) * CHUNK] * dt_t[h : h + 1, :] * decays
                d_scores = d_scores + pull
                kernels.append((pull * scores).astype(BF))
            pulls.append(mm_at(jnp.concatenate(mixing, axis=0), stacked))
        d_scaled = jnp.concatenate(pulls, axis=1) + from_state
        per_head = mm_fine(
            jnp.concatenate(
                [row_enter, exits, values_f * d_scaled, jnp.broadcast_to(through_sum, (8, cd))],
                axis=0,
            ),
            gather,
            2,
        )
        row_enter = per_head[:CHUNK]
        exits = per_head[CHUNK : 2 * CHUNK]
        d_dt = per_head[2 * CHUNK : 3 * CHUNK]
        passing = per_head[3 * CHUNK : 3 * CHUNK + 1]
        row_sums = mm(jnp.concatenate(kernels, axis=1), pick_head)
        col_sums = mm_at(jnp.concatenate(kernels, axis=0), pick_head)
        d_rate = (
            mm_fine_right(from_here, row_sums - col_sums + row_enter, 3)
            + mm_fine_right(before, exits, 3)
            + passing
        )
        d_raw = (d_dt - d_rate * decay_row) * jax.nn.sigmoid(raw)
        head_sums[0:1, :] += jnp.sum(d_raw, axis=0, keepdims=True)
        head_sums[1:2, :] += jnp.sum(d_rate * rate, axis=0, keepdims=True)
        d_scores_b = d_scores.astype(BF)
        d_readers = d_readers + mm(d_scores_b, writers)
        d_writers = d_writers + mm_at(d_scores_b, readers)
        d_values = dt_w * d_scaled + skip_row * dy
        ext[at, :] = jnp.concatenate([d_values, d_writers, d_readers], axis=1) * d_silu[at]
        out_buf[at, cd + conv_ch :] = d_raw.astype(BF)
    conv_in = mixed_ref[0, :, cd : cd + conv_ch]
    d_conv = jnp.zeros((rows, conv_ch), F32)
    for j in range(4):
        part = ext[pl.ds(j, rows), :]
        if j:
            part = jnp.where(age_ext[j : j + rows, :] >= j, part, 0.0)
        else:
            wide_sums[4:5, :] += jnp.sum(part, axis=0, keepdims=True)
        d_conv = d_conv + pc_ref[3 - j : 4 - j, :] * part
        wide_sums[3 - j : 4 - j, :] += jnp.sum(part * conv_in, axis=0, keepdims=True)
    out_buf[:, cd : cd + conv_ch] = d_conv.astype(BF)
    mixed_grad_ref[0] = out_buf[...]
    weight = weight_ref[...].reshape(-1, weight_ref.shape[2])
    unit_grad = mm_bt(out_buf[...], weight).astype(BF)
    unit_grad_buf = refs[-1]
    unit_grad_buf[...] = unit_grad.reshape(unit_grad_buf.shape)
    for k in range(count):
        unit_grad_ref[k, 0] = unit_grad_buf[jnp.bitwise_xor(shift, k)]


def whole(shape):
    return pl.BlockSpec(shape, lambda *_: (0,) * len(shape), pipeline_mode=pl.Buffered(1))


def mixer_forward(shift, units, weight, ordered, age, pc, ph):
    count = len(units)
    blocks, q, model = units[0].shape
    width = weight.shape[2]
    weight_block = (weight.shape[0], model // weight.shape[0], width)
    conv_ch = pc.shape[1]
    cd = conv_ch - 2 * STATE
    rows = count * q
    chunks = rows // CHUNK
    in_specs = shard_specs(count, blocks, q, model, lambda i, s: i ^ s[1]) + [
        whole(weight_block),
        pl.BlockSpec((1, rows + HALO, 1), lambda i, s: (i, 0, 0)),
        whole(pc.shape),
        whole(ph.shape),
    ]

    def in_order(*shape):
        return pl.BlockSpec((1,) + shape, lambda i, s: (i,) + (0,) * len(shape))

    def relative(last):
        return pl.BlockSpec((count, 1, q, last), lambda i, s: (0, i ^ s[1], 0, 0))

    return pl.pallas_call(
        partial(forward_kernel, count=count, cd=cd, ordered=ordered),
        out_shape=[
            jax.ShapeDtypeStruct((blocks, rows, model), BF),
            jax.ShapeDtypeStruct((blocks, rows, width), F32),
            jax.ShapeDtypeStruct((count, blocks, q, cd), BF),
            jax.ShapeDtypeStruct((blocks, rows, conv_ch), F32),
            jax.ShapeDtypeStruct((blocks, rows, cd), F32),
            jax.ShapeDtypeStruct((blocks, chunks, STATE, cd), BF),
            jax.ShapeDtypeStruct((count, blocks, q, LANES), BF),
        ],
        grid_spec=pltpu.PrefetchScalarGridSpec(
            num_scalar_prefetch=1,
            grid=(blocks,),
            in_specs=in_specs,
            out_specs=[
                in_order(rows, model),
                in_order(rows, width),
                relative(cd),
                in_order(rows, conv_ch),
                in_order(rows, cd),
                in_order(chunks, STATE, cd),
                relative(LANES),
            ],
            scratch_shapes=[
                pltpu.VMEM((count, q, model), BF),
                pltpu.VMEM((count, q, cd), BF),
                pltpu.VMEM((rows + HALO, conv_ch), F32),
                pltpu.VMEM((STATE, cd), F32),
                pltpu.VMEM((count, q, LANES), BF),
            ],
        ),
        compiler_params=pltpu.CompilerParams(vmem_limit_bytes=52 * 2**20),
        cost_estimate=pl.CostEstimate(
            flops=2 * 10**10, bytes_accessed=4 * 10**7, transcendentals=10**6
        ),
    )(shift, *flat_shards(units), weight, age, pc, ph)


def flat_shards(shards):
    out = []
    for shard in shards:
        out += list(shard) if isinstance(shard, tuple) else [shard]
    return out


def mixer_backward(
    shift, grads, scales, weight_out, weight, mixed, age, pc, ph, pre, ssd, states, model
):
    blocks, rows, width = mixed.shape
    weight_block = (weight.shape[0], model // weight.shape[0], width)
    conv_ch = pc.shape[1]
    cd = conv_ch - 2 * STATE
    chunks = rows // CHUNK
    top = blocks - 1
    if scales is not None:
        count, _, q, _ = grads.shape
        in_specs = [
            pl.BlockSpec((count, 1, q, cd), lambda i, s: (0, (top - i) ^ s[1], 0, 0)),
            pl.BlockSpec((count, 1, q, 2), lambda i, s: (0, (top - i) ^ s[1], 0, 0)),
        ]
        args = [grads, scales]
    else:
        count = len(grads)
        _, q, grad_width = grads[0].shape
        in_specs = shard_specs(count, blocks, q, grad_width, lambda i, s: (top - i) ^ s[1])
        in_specs.append(whole(weight_out.shape))
        args = flat_shards(grads) + [weight_out]

    def in_order(*shape):
        return pl.BlockSpec((1,) + shape, lambda i, s: (top - i,) + (0,) * len(shape))

    in_specs += [
        whole(weight_block),
        in_order(rows, width),
        in_order(rows + HALO, 1),
        whole(pc.shape),
        whole(ph.shape),
        in_order(rows, conv_ch),
        in_order(rows, cd),
        in_order(chunks, STATE, cd),
    ]
    args += [weight, mixed, age, pc, ph, pre, ssd, states]
    scratch = [
        pltpu.VMEM((rows, width), BF),
        pltpu.VMEM((rows + HALO, conv_ch), F32),
        pltpu.VMEM((STATE, cd), F32),
    ]
    if scales is None:
        scratch.append(pltpu.VMEM((count, q, grad_width), BF))
    scratch.append(pltpu.VMEM((count, q, model), BF))
    return pl.pallas_call(
        partial(backward_kernel, count=count, cd=cd, own_scales=scales is not None),
        out_shape=[
            jax.ShapeDtypeStruct((blocks, rows, width), BF),
            jax.ShapeDtypeStruct((count, blocks, q, model), BF),
            jax.ShapeDtypeStruct((8, conv_ch), F32),
            jax.ShapeDtypeStruct((8, LANES), F32),
        ],
        grid_spec=pltpu.PrefetchScalarGridSpec(
            num_scalar_prefetch=1,
            grid=(blocks,),
            in_specs=in_specs,
            out_specs=[
                in_order(rows, width),
                pl.BlockSpec((count, 1, q, model), lambda i, s: (0, (top - i) ^ s[1], 0, 0)),
                pl.BlockSpec((8, conv_ch), lambda i, s: (0, 0)),
                pl.BlockSpec((8, LANES), lambda i, s: (0, 0)),
            ],
            scratch_shapes=scratch,
        ),
        compiler_params=pltpu.CompilerParams(vmem_limit_bytes=52 * 2**20),
        cost_estimate=pl.CostEstimate(
            flops=4 * 10**10, bytes_accessed=5 * 10**7, transcendentals=2 * 10**6
        ),
    )(shift, *args)


SMALL_ROWS = 16


def shard_kernel(at_ref, *refs, cd, hd, small):
    gate_ref, values_ref, rest_ref, step_ref, gain_ref, refs = *refs[:5], refs[5:]
    gain = gain_ref[...]
    rows = gain.shape[0]
    conv_ch = cd + 2 * STATE

    def scaled(ref):
        return (ref[0].astype(F32) * gain).astype(BF)

    out_ref = refs[small]
    out_ref[0:rows, :cd] = scaled(gate_ref)
    out_ref[0:rows, cd : 2 * cd] = scaled(values_ref)
    out_ref[0:rows, 2 * cd : cd + conv_ch] = scaled(rest_ref)
    steps = step_ref[0]
    shape = (steps.shape[0], LANES)
    heads, cols = iota2(shape, 0), iota2(shape, 1)
    chosen = ((heads == at_ref[0] * hd + cols) & (cols < hd)).astype(BF)
    out_ref[0:rows, cd + conv_ch :] = (mm_at(steps, chosen) * gain).astype(BF)
    if small:
        buf = refs[small + 1]
        buf[...] = jnp.zeros_like(buf)
        at, lane = 0, 0
        for ref in refs[:small]:
            count, lanes = ref.shape
            buf[at : at + count, lane : lane + lanes] = ref[...].astype(F32)
            if lanes < LANES:
                lane += LANES
            else:
                at += count
        out_ref[rows : rows + SMALL_ROWS, :] = buf[...].astype(BF)


def weight_shard(shift, layer, input_proj, step_proj, gain, cd, hd, small=()):
    _, rows, columns = input_proj.shape
    heads = step_proj.shape[1]
    parts = heads // hd
    at_rest = (columns - 2 * STATE) // (2 * STATE)
    width = 2 * cd + 2 * STATE + LANES
    full = rows + SMALL_ROWS if small else rows
    return pl.pallas_call(
        partial(shard_kernel, cd=cd, hd=hd, small=len(small)),
        out_shape=jax.ShapeDtypeStruct((full, width), BF),
        grid_spec=pltpu.PrefetchScalarGridSpec(
            num_scalar_prefetch=1,
            grid=(1,),
            in_specs=[
                pl.BlockSpec((1, rows, cd), lambda i, s: (layer, 0, s[0])),
                pl.BlockSpec((1, rows, cd), lambda i, s: (layer, 0, parts + s[0])),
                pl.BlockSpec((1, rows, 2 * STATE), lambda i, s: (layer, 0, at_rest)),
                pl.BlockSpec((1, heads, rows), lambda i, s: (layer, 0, 0)),
                whole((rows, 1)),
            ]
            + [whole(x.shape) for x in small],
            out_specs=pl.BlockSpec((full, width), lambda i, s: (0, 0)),
            scratch_shapes=[pltpu.VMEM((SMALL_ROWS, width), F32)] if small else [],
        ),
        cost_estimate=pl.CostEstimate(flops=10**6, bytes_accessed=2 * 10**6, transcendentals=0),
    )(shift, input_proj, input_proj, input_proj, step_proj, gain[:, None], *small)


def place_kernel(shift_ref, *refs, count, dim):
    out_ref = refs[count]
    for k in range(count):
        at = (slice(None),) * dim + (jnp.bitwise_xor(shift_ref[0], k),)
        out_ref[at] = refs[k][...]


def place(shift, parts, dim):
    shape = parts[0].shape
    full = shape[:dim] + (len(parts),) + shape[dim:]
    return pl.pallas_call(
        partial(place_kernel, count=len(parts), dim=dim),
        out_shape=jax.ShapeDtypeStruct(full, parts[0].dtype),
        grid_spec=pltpu.PrefetchScalarGridSpec(
            num_scalar_prefetch=1,
            grid=(1,),
            in_specs=[whole(part.shape) for part in parts],
            out_specs=whole(full),
        ),
        compiler_params=pltpu.CompilerParams(vmem_limit_bytes=40 * 2**20),
        cost_estimate=pl.CostEstimate(flops=0, bytes_accessed=5 * 10**6, transcendentals=0),
    )(shift, *parts)


def finish_kernel(shift_ref, *refs, count, cd, inner, rows, out_part, apart):
    part_refs, refs = refs[:count], refs[count:]
    own_refs, refs = (refs[:count], refs[count:]) if apart else (None, refs)
    weight_ref, gain_ref, refs = refs[0], refs[1], refs[2:]
    grad_ref, out_ref, norm_ref = refs[-3:]
    gain = gain_ref[...]
    norm = jnp.zeros((rows, 1), F32)

    def put(at, value, norm):
        cols = pl.ds(at, value.shape[1])
        grad_ref[0, :, cols] = value * gain
        return norm + jnp.sum(
            value * weight_ref[0, :, cols].astype(F32), axis=1, keepdims=True
        )

    rest = jnp.zeros((rows, 2 * STATE), F32)
    for k in range(count):
        j = jnp.bitwise_xor(shift_ref[0], k)
        part = part_refs[k][:rows, :].astype(F32)
        norm = put(pl.multiple_of(j * cd, LANES), part[:, :cd], norm)
        norm = put(pl.multiple_of(inner + j * cd, LANES), part[:, cd : 2 * cd], norm)
        rest = rest + part[:, 2 * cd : 2 * cd + 2 * STATE]
        own = (own_refs[k][...] if apart else part_refs[k][rows:, :]).astype(F32)
        out_ref[0, pl.ds(pl.multiple_of(j * out_part, 8), out_part), :] = own[
            :out_part, : out_ref.shape[2]
        ]
    norm_ref[...] = put(2 * inner, rest, norm)


def finish(layer, shift, parts, apart, weight, gain, out_part, out_cols, before, cd, inner):
    count = len(parts)
    layers, rows, columns = weight.shape
    in_specs = [whole(part.shape) for part in parts + (apart or [])] + [
        pl.BlockSpec((1, rows, columns), lambda i, s: (layer, 0, 0)),
        whole((rows, 1)),
    ]
    args = parts + (apart or []) + [weight, gain[:, None]]
    aliases = {}
    if before is not None:
        aliases = {len(args) + 1: 0, len(args) + 2: 1}
        in_specs += [pl.BlockSpec(memory_space=pl.ANY)] * 2
        args += list(before)
    return pl.pallas_call(
        partial(
            finish_kernel,
            count=count,
            cd=cd,
            inner=inner,
            rows=rows,
            out_part=out_part,
            apart=apart is not None,
        ),
        out_shape=[
            jax.ShapeDtypeStruct((layers, rows, columns), F32),
            jax.ShapeDtypeStruct((layers, count * out_part, out_cols), F32),
            jax.ShapeDtypeStruct((rows, 1), F32),
        ],
        grid_spec=pltpu.PrefetchScalarGridSpec(
            num_scalar_prefetch=1,
            grid=(1,),
            in_specs=in_specs,
            out_specs=[
                pl.BlockSpec((1, rows, columns), lambda i, s: (layer, 0, 0)),
                pl.BlockSpec((1, count * out_part, out_cols), lambda i, s: (layer, 0, 0)),
                whole((rows, 1)),
            ],
        ),
        input_output_aliases=aliases,
        compiler_params=pltpu.CompilerParams(vmem_limit_bytes=48 * 2**20),
        cost_estimate=pl.CostEstimate(flops=10**7, bytes_accessed=2 * 10**7, transcendentals=0),
    )(shift, *args)


def swap(value, axis, k, size):
    return lax.ppermute(value, axis, [(i, i ^ k) for i in range(size)])


def pick(value, index):
    return lax.dynamic_index_in_dim(value, index, 0, keepdims=False)


def tie(*values):
    return lax.optimization_barrier(values)


def after(value, *first):
    return lax.optimization_barrier((value, first))[0]


def sends(parts, base, size):
    return [pick(parts, base ^ k) for k in range(size)]


def moved(items, axis, what):
    size = len(items)
    with jax.named_scope(what):
        return [items[0]] + [swap(items[k], axis, k, size) for k in range(1, size)]


def gather_rows(shard, n, what, arrived=None):
    if n != 4:
        everything = lax.all_gather(shard, "dp")
        mine = lax.axis_index("dp")
        return [pick(everything, mine ^ k) for k in range(n)], arrived
    half = shard.shape[0] // 2
    with jax.named_scope(what):
        first = swap(shard, "dp", 1, n)
        second = swap(shard, "dp", 2, n)
        if arrived is not None:
            first, second, arrived = tie(first, second, arrived)
        low = swap(first[:half], "dp", 2, n)
        high = swap(second[half:], "dp", 1, n)
    return [shard, first, second, (low, high)], arrived


def joined(shards):
    return [
        jnp.concatenate(shard, axis=0) if isinstance(shard, tuple) else shard for shard in shards
    ]


def reduce_rows(parts, n, what, during=None):
    with jax.named_scope(what):
        return reduce_parts(parts, n, during)


def reduce_parts(parts, n, during=None):
    if n != 4:
        mine = lax.axis_index("dp")
        ordered = jnp.stack([pick(parts, mine ^ j) for j in range(n)])
        total = lax.psum_scatter(ordered, "dp", scatter_dimension=0, tiled=False).astype(F32)
        return (total, None if during is None else during[0](*during[1]))
    half = parts.shape[1] // 2
    a, b = parts[:, :half], parts[:, half:]
    send_a, send_b = tie(jnp.stack([a[1], a[3]]), jnp.stack([b[2], b[3]]))
    got_a = swap(send_a, "dp", 1, n)
    got_b = swap(send_b, "dp", 2, n)
    work = None
    if during is not None:
        function, args = during
        work = function(*after(args, send_a, send_b))
        got_a, got_b, work = tie(got_a, got_b, work)
    on_a = (a[2].astype(F32) + got_a[1].astype(F32)).astype(BF)
    on_b = (b[1].astype(F32) + got_b[1].astype(F32)).astype(BF)
    last_a = swap(on_a, "dp", 2, n)
    last_b = swap(on_b, "dp", 1, n)
    sum_a = a[0].astype(F32) + got_a[0].astype(F32) + last_a.astype(F32)
    sum_b = b[0].astype(F32) + got_b[0].astype(F32) + last_b.astype(F32)
    return jnp.concatenate([sum_a, sum_b], axis=0), work


def both_cores(block, what):
    core = lax.axis_index("core")
    keep = pick(block, core)
    with jax.named_scope(what):
        other = lax.ppermute(pick(block, 1 - core), "core", [(0, 1), (1, 0)])
    first = jnp.where(core == 0, keep, other)
    second = jnp.where(core == 0, other, keep)
    return jnp.concatenate([first, second], axis=0)


def to_groups(both, n, what):
    q = both.shape[0] // n
    d = lax.axis_index("dp")
    return jnp.stack(moved(sends(both.reshape(n, q, -1), d, n), "dp", what))


def to_chunks(groups, z_count, what):
    d, z = lax.axis_index("dp"), lax.axis_index("z")
    return jnp.stack(moved(sends(groups, z ^ d, z_count), "z", what))


def from_groups(groups, n, what):
    d, z = lax.axis_index("dp"), lax.axis_index("z")
    return jnp.stack(moved(sends(groups, z ^ d, n), "dp", what))


def from_both(parts, what):
    n = parts.shape[0]
    d, core = lax.axis_index("dp"), lax.axis_index("core")
    half = n // 2

    def side(c):
        return jnp.concatenate([pick(parts, (half * c + i) ^ d) for i in range(half)], axis=0)

    with jax.named_scope(what):
        other = lax.ppermute(side(1 - core), "core", [(0, 1), (1, 0)])
    keep = side(core)
    return jnp.stack([jnp.where(core == 0, keep, other), jnp.where(core == 0, other, keep)])


def on_device(
    hidden_in,
    doc_lengths,
    norm_gain,
    input_proj,
    step_proj,
    conv_weight,
    conv_bias,
    step_bias,
    decay_log,
    skip_gain,
    gate_gain,
    output_proj,
    cotangent,
    *,
    n,
    z_count,
):
    layers = norm_gain.shape[0]
    owners = 2 * z_count
    d_rows = norm_gain.shape[1]
    width_d = d_rows * owners
    heads_f = step_bias.shape[1]
    heads = heads_f * owners
    hd = heads // n
    cd = hd * HEAD_DIM
    inner = heads * HEAD_DIM
    conv_f = conv_bias.shape[1]
    conv_ch = cd + 2 * STATE
    gate_f = gate_gain.shape[1]
    out_rows = output_proj.shape[1]
    width_in = cd + conv_ch + LANES
    step_at = cd + conv_ch
    d = lax.axis_index("dp")
    z = lax.axis_index("z")
    core = lax.axis_index("core")
    shift = jnp.stack([d, z]).astype(jnp.int32)

    small_len = 5 * conv_f + gate_f + 3 * heads_f
    small_cols = -(-small_len // d_rows)

    def small_split(flat):
        sizes = (4 * conv_f, conv_f, gate_f, heads_f, heads_f, heads_f)
        parts, at = [], 0
        for size in sizes:
            parts.append(flat[..., at : at + size])
            at += size
        return parts

    small_lanes = max(-(-max(conv_f, gate_f) // LANES), 3) * LANES

    def small_unpack(everything):
        everything = everything.astype(F32)

        def rows(at, count, lanes):
            part = everything[:, at : at + count, lanes]
            return part.transpose(1, 0, 2).reshape(count, -1)

        def mine(x):
            width = x.shape[1] // n
            return lax.dynamic_slice_in_dim(x, d * width, width, 1)

        conv = rows(0, 5 * layers, slice(0, conv_f))
        conv = jnp.concatenate([mine(conv[:, :inner]), conv[:, inner:]], axis=1)
        gain = mine(rows(5 * layers, layers, slice(0, gate_f)))
        at = 6 * layers
        bias, decay, skip = (
            mine(rows(at, layers, slice(i * LANES, i * LANES + heads_f))) for i in range(3)
        )
        skip = jnp.broadcast_to(skip[:, :, None], (layers, hd, HEAD_DIM)).reshape(layers, cd)
        wide = jnp.pad(jnp.stack([skip, gain], axis=1), ((0, 0), (0, 1), (0, 2 * STATE)))
        head = jnp.stack([bias, jnp.exp(decay)], axis=1)
        head = jnp.pad(head, ((0, 0), (0, 6), (0, LANES - hd)))
        pcs = [
            jnp.concatenate(
                [conv[4 * l : 4 * l + 4], conv[4 * layers + l : 4 * layers + l + 1], wide[l]],
                axis=0,
            )
            for l in range(layers)
        ]
        return pcs, [head[l] for l in range(layers)]

    out_part = out_rows // n

    def shard_out(layer):
        return lax.dynamic_slice_in_dim(output_proj[layer], d * out_part, out_part, 0)

    def column_sends(column):
        return sends(column.reshape(n, 2, out_part, width_d), d, n)

    def weight_out(parts):
        return place(shift, parts, 1).reshape(cd, width_d)

    def grad_out_sends(d_out):
        return sends(d_out.reshape(2, n, out_part, width_d).transpose(1, 0, 2, 3), d, n)

    def grad_out_owned(by_rows):
        rows_all = place(shift, by_rows, 0).reshape(owners, out_part, width_d)
        return lax.psum_scatter(rows_all, PLANE, scatter_dimension=0)

    def small_out(wide_sums, head_sums):
        conv_full = jnp.concatenate([jnp.zeros((5, inner), F32), wide_sums[:5, cd:]], axis=1)
        conv_full = lax.dynamic_update_slice(conv_full, wide_sums[:5, :cd], (0, d * cd))
        conv_full = conv_full.reshape(5, owners, conv_f).transpose(1, 0, 2).reshape(owners, -1)
        gain_full = lax.dynamic_update_slice(jnp.zeros((inner,), F32), wide_sums[6, :cd], (d * cd,))
        skip_sum = jnp.sum(wide_sums[5, :cd].reshape(hd, HEAD_DIM), axis=1)
        head_full = lax.dynamic_update_slice(
            jnp.zeros((3, heads), F32),
            jnp.stack([head_sums[0, :hd], head_sums[1, :hd], skip_sum]),
            (0, d * hd),
        )
        head_full = head_full.reshape(3, owners, heads_f).transpose(1, 0, 2).reshape(owners, -1)
        small = jnp.concatenate([conv_full, gain_full.reshape(owners, gate_f), head_full], axis=1)
        small = jnp.pad(small, ((0, 0), (0, small_cols * d_rows - small_len)))
        return small.reshape(owners * d_rows, small_cols)

    def grad_in(unit_cat, d_mixed, wide_sums, head_sums):
        small = small_out(wide_sums, head_sums)
        product = mm_at(flat(unit_cat), flat(d_mixed))
        return (
            product + jnp.pad(small, ((0, 0), (step_at + hd, LANES - hd - small_cols)))
        ).astype(BF)

    out_padded = -(-out_part // 16) * 16

    def owned_parts(own_in, own_out, what):
        own_out = jnp.pad(own_out, ((0, out_padded - out_part), (0, 0)))
        if width_in < width_d:
            return joined(gather_rows(own_in, n, what)[0]), joined(gather_rows(own_out, n, what)[0])
        own_out = jnp.pad(own_out, ((0, 0), (0, width_in - width_d)))
        return joined(gather_rows(jnp.concatenate([own_in, own_out], axis=0), n, what)[0]), None

    def finished_layer(layer, owned, before):
        parts, apart = owned
        at = slice(step_at + hd, step_at + hd + small_cols)
        small = sum(part[:d_rows, at].astype(F32) for part in parts)
        small = small_split(small.reshape(-1)[:small_len])
        steps = jnp.stack([part[:d_rows, step_at : step_at + hd] for part in parts])
        steps = jnp.stack([pick(steps, d ^ j) for j in range(n)]).astype(F32)
        steps = steps.transpose(0, 2, 1).reshape(heads, d_rows)
        gain = norm_gain[layer].astype(F32)
        in_all, out_all, norm_grad = finish(
            layer, shift, parts, apart, input_proj, gain, out_part, width_d, before, cd, inner
        )
        norm_grad = norm_grad[:, 0] + jnp.sum(steps * step_proj[layer].astype(F32), axis=0)
        rest = (
            norm_grad,
            steps * gain[None, :],
            small[0].reshape(4, conv_f),
            small[1],
            small[3],
            small[4],
            small[5],
            small[2],
        )
        return (in_all, out_all), rest

    both = lax.ppermute(
        doc_lengths,
        ("dp", "z"),
        [(i * z_count + j, j * z_count + i) for i in range(n) for j in range(z_count)],
    )
    ends = jnp.cumsum(pick(both, core))
    tok = hidden_in.shape[1]
    block_rows = 2 * tok
    row_len = block_rows * z_count
    q = block_rows // n
    positions = jnp.arange(row_len, dtype=jnp.int32)
    begin = jnp.max(jnp.where(ends[None, :] <= positions[:, None], ends[None, :], 0), axis=1)
    age = (positions - begin).reshape(z_count, block_rows)
    follow = jnp.concatenate([age[1:, :HALO], jnp.zeros((1, HALO), jnp.int32)], axis=0)
    age = jnp.concatenate([age, follow], axis=1)[:, :, None]

    def normalize(resid):
        inv = lax.rsqrt(jnp.mean(resid * resid, axis=-1, keepdims=True) + EPSILON)
        return inv, resid * inv

    def flat(x):
        return x.reshape(-1, x.shape[-1])

    def norm_back(back, resid, inv, normed_grad):
        u = resid * inv
        return back + inv * (
            normed_grad - u * jnp.mean(normed_grad * u, axis=-1, keepdims=True)
        )

    both = both_cores(hidden_in, "hidden_cores")
    small = (
        conv_weight.reshape(layers * 4, conv_f),
        conv_bias,
        gate_gain,
        step_bias,
        decay_log,
        skip_gain,
    )
    shard0 = weight_shard(
        shift, 0, input_proj, step_proj, norm_gain[0].astype(F32), cd, hd, small
    )
    both, shard0 = tie(both, shard0)
    w_in0 = lax.all_gather(shard0, PLANE)
    groups = to_groups(both, n, "hidden_groups")
    resid0 = to_chunks(groups, z_count, "hidden_chunks").astype(F32)
    inv0, unit = normalize(resid0)
    unit = unit.astype(BF)
    shard1 = weight_shard(shift, 1, input_proj, step_proj, norm_gain[1].astype(F32), cd, hd)
    shard_out0, shard1, shard_out1, unit = tie(shard_out(0), shard1, shard_out(1), unit)
    column0 = lax.all_gather(shard_out0, PLANE)
    w_in1 = lax.all_gather(shard1, PLANE)
    column1 = lax.all_gather(shard_out1, PLANE)
    units0, w_in0 = gather_rows(unit, n, "unit0", w_in0)
    pcs, phs = small_unpack(w_in0[:, d_rows:, :small_lanes])

    items, w_in0 = tie(column_sends(after(column0, *flat_shards(units0))), w_in0)
    parts = moved(items, "dp", "weight_out0")
    _, mixed0, gated0, pre0, ssd0, states0, sums0 = layer0 = mixer_forward(
        shift, units0, w_in0, False, age, pcs[0], phs[0]
    )
    unit_cat0 = layer0[0]
    parts, gated0 = tie(parts, gated0)
    w_out0 = weight_out(parts)
    sent = mm(flat(gated0), w_out0).astype(BF).reshape(n, z_count, q, width_d)
    sent = jnp.concatenate([sent, sums0], axis=-1)
    cot_both = both_cores(after(cotangent, sent), "cot_cores")
    cot_items = sends(cot_both.reshape(n, q, width_d), d, n)
    cot_groups = moved(cot_items, "dp", "cot_groups")
    got, _ = reduce_rows(sent, n, "product0")
    squares = jnp.sum(got[..., width_d:], axis=-1, keepdims=True)
    ginv0 = lax.rsqrt(squares / inner + EPSILON)
    branch0 = got[..., :width_d] * ginv0
    resid1 = resid0 + branch0

    inv1, unit = normalize(resid1)
    unit, *cot_groups = tie(unit.astype(BF), *cot_groups)
    cot_chunks = moved(sends(jnp.stack(cot_groups), z ^ d, z_count), "z", "cot_chunks")
    units1, _ = gather_rows(unit, n, "unit1")
    cot_chunks, units1 = tie(cot_chunks, units1)
    upstream = jnp.stack(cot_chunks)
    items, w_in1 = tie(column_sends(after(column1, *flat_shards(units1))), w_in1)
    parts = moved(items, "dp", "weight_out1")
    unit_cat1, mixed1, gated1, pre1, ssd1, states1, sums1 = mixer_forward(
        shift, units1, w_in1, True, age, pcs[1], phs[1]
    )
    upstream_parts, gated1 = gather_rows(upstream, n, "upstream", gated1)
    parts, gated1 = tie(parts, gated1)
    upstream_all = place(shift, joined(upstream_parts), 0)
    w_out1 = weight_out(parts)
    gg1 = mm_bt(flat(upstream_all), w_out1).reshape(n, z_count, q, cd)
    s1 = jnp.sum(sums1.astype(F32), axis=-1)
    s2 = jnp.sum(gg1 * gated1.astype(F32), axis=-1)
    totals = jnp.stack([s1, s2]).reshape(2, row_len // LANES, LANES)
    bit = 1
    while bit < n:
        with jax.named_scope("totals"):
            totals = totals + swap(totals, "dp", bit, n)
        bit *= 2
    totals = totals.reshape(2, n, z_count, q)
    ginv1 = lax.rsqrt(totals[0] / inner + EPSILON)
    scales = jnp.stack([ginv1, ginv1 * ginv1 * ginv1 * totals[1] / inner], axis=-1)
    relative1 = jnp.stack([pick(gated1, d ^ k) for k in range(n)])
    sent1 = mm(flat(relative1), w_out1).astype(BF).reshape(n, z_count, q, width_d)
    own = pick(ginv1, d)[..., None]

    weighted = (gated1.astype(F32) * ginv1[..., None]).astype(BF)
    d_out1 = mm_at(flat(weighted), flat(upstream_all)).astype(BF)
    items, sent1, gg1 = tie(grad_out_sends(d_out1), sent1, gg1)
    by_rows = moved(items, "dp", "grad_out1")

    def backward1(gg1):
        return mixer_backward(
            shift, gg1, scales, None, w_in1, mixed1, age, pcs[1], phs[1], pre1, ssd1, states1,
            width_d,
        )

    total1, (d_mixed, sent, wide_sums, head_sums) = reduce_rows(
        sent1, n, "product1", (backward1, (gg1,))
    )
    by_rows, sent = tie(by_rows, sent)
    own_out1 = grad_out_owned(by_rows)
    normed_grad, d_in1 = reduce_rows(
        sent, n, "back1", (grad_in, (unit_cat1, d_mixed, wide_sums, head_sums))
    )
    own_in1 = lax.psum_scatter(d_in1, PLANE, scatter_dimension=0, tiled=True)
    back1 = norm_back(upstream.astype(F32), resid1, inv1, normed_grad)

    low = back1.astype(BF).astype(F32)
    mean = jnp.sum(low * branch0, axis=-1, keepdims=True) / inner
    kappa = ginv0 * ginv0 * mean
    high = kappa.astype(BF)
    rest = (kappa - high.astype(F32)).astype(BF)
    payload = jnp.concatenate(
        [(low * ginv0).astype(BF), high, rest, jnp.zeros((z_count, q, LANES - 2), BF)], axis=-1
    )
    hidden_out = (resid1 + after(total1, payload) * own).astype(BF)
    out_chunks = moved([hidden_out[k] for k in range(z_count)], "z", "hidden_out_chunks")
    g_all, _ = gather_rows(payload, n, "branch_grad0")
    out_chunks, g_all = tie(out_chunks, g_all)
    d_out0 = mm_at(flat(gated0), flat(jnp.stack(joined(g_all)))[:, :width_d]).astype(BF)
    items, g_all = tie(grad_out_sends(d_out0), g_all)
    by_rows = moved(items, "dp", "grad_out0")
    d_mixed, sent, wide_sums, head_sums = mixer_backward(
        shift, g_all, None, w_out0, w_in0, mixed0, age, pcs[0], phs[0], pre0, ssd0, states0,
        width_d,
    )
    by_rows, sent = tie(by_rows, sent)
    own_out0 = grad_out_owned(by_rows)
    normed_grad, d_in0 = reduce_rows(
        sent, n, "back0", (grad_in, (unit_cat0, d_mixed, wide_sums, head_sums))
    )
    own_in0 = lax.psum_scatter(d_in0, PLANE, scatter_dimension=0, tiled=True)
    back0 = norm_back(back1, resid0, inv0, normed_grad).astype(BF)
    own_in1, own_out1, back0 = tie(own_in1, own_out1, back0)
    back_chunks = moved([back0[k] for k in range(z_count)], "z", "back_chunks")
    owned1 = owned_parts(own_in1, own_out1, "owned1")
    back_chunks, owned1 = tie(back_chunks, owned1)
    back_groups = from_groups(jnp.stack(back_chunks), n, "back_groups")
    buffers, rest1 = finished_layer(1, owned1, None)
    back_groups, buffers = tie(back_groups, buffers)
    hidden_grad = from_both(back_groups, "back_cores").astype(F32)
    out_groups = from_groups(jnp.stack(after(out_chunks, back_groups)), n, "hidden_out_groups")
    hidden_out = from_both(out_groups, "hidden_out_cores")
    own_in0, own_out0, buffers, out_groups = tie(own_in0, own_out0, buffers, out_groups)
    owned0 = owned_parts(own_in0, own_out0, "owned0")
    buffers, rest0 = finished_layer(0, owned0, buffers)
    stacked = tuple(jnp.stack([first, second]) for first, second in zip(rest0, rest1))
    return (hidden_out, hidden_grad, stacked[0], buffers[0], *stacked[1:], buffers[1])


def solution(mesh):
    n = mesh.shape["dp"]
    z_count = mesh.shape["fsdp"] // 2
    assert n == z_count
    split = Mesh(mesh.devices.reshape(n, z_count, 2), ("dp", "z", "core"))
    fsdp = PLANE
    tokens = P("dp", fsdp, None)
    last = P(None, fsdp)
    weights = (
        last,
        P(None, fsdp, None),
        P(None, None, fsdp),
        P(None, None, fsdp),
        last,
        last,
        last,
        last,
        last,
        P(None, fsdp, None),
    )
    return jax.shard_map(
        partial(on_device, n=n, z_count=z_count),
        mesh=split,
        in_specs=(tokens, P("dp", None)) + weights + (tokens,),
        out_specs=(tokens, tokens) + weights,
        check_vma=False,
    )
```

```python
from functools import partial

import jax
import jax.numpy as jnp
from jax import lax
from jax.experimental import pallas as pl
from jax.experimental.pallas import tpu as pltpu
from jax.sharding import Mesh
from jax.sharding import PartitionSpec as P

BF = jnp.bfloat16
F32 = jnp.float32
HIGHEST = lax.Precision.HIGHEST
EPSILON = 1e-05
HEAD_DIM = 64
STATE = 128
LANES = 128
CHUNK = 128
HALO = 8
FAR = -1e30
PLANE = ("z", "core")


def mm(a, b):
    return lax.dot_general(a, b, (((1,), (0,)), ((), ())), preferred_element_type=F32)


def mm_bt(a, b):
    return lax.dot_general(a, b, (((1,), (1,)), ((), ())), preferred_element_type=F32)


def mm_at(a, b):
    return lax.dot_general(a, b, (((0,), (0,)), ((), ())), preferred_element_type=F32)


def halves(x, count):
    out = []
    for _ in range(count):
        part = x.astype(BF)
        out.append(part)
        x = x - part.astype(F32)
    return out


def mm_fine(a, b, count):
    return sum(mm(part, b) for part in halves(a, count))


def mm_fine_right(a, b, count):
    return sum(mm(a, part) for part in halves(b, count))


def iota2(shape, dim):
    return lax.broadcasted_iota(jnp.int32, shape, dim)


def head_spread(width):
    return (iota2((LANES, width), 1) // HEAD_DIM == iota2((LANES, width), 0)).astype(BF)


def head_gather(width):
    return (iota2((width, LANES), 0) // HEAD_DIM == iota2((width, LANES), 1)).astype(BF)


def softplus(x):
    return jnp.maximum(x, 0.0) + jnp.log1p(jnp.exp(-jnp.abs(x)))


def chunk_terms(step, age, bias_row, decay_row):
    raw = step + bias_row
    dt = softplus(raw)
    rate = -dt * decay_row
    rows = iota2((CHUNK, CHUNK), 0)
    cols = iota2((CHUNK, CHUNK), 1)
    lower = (cols <= rows).astype(BF)
    total = mm_fine_right(lower, rate, 3)
    pos = iota2((CHUNK, 1), 0)
    first = pos - age
    bias = jnp.where((cols <= rows) & (cols >= first), 0.0, FAR)
    first_last = first[CHUNK - 1 :, :]
    enter = jnp.exp(total) * (first < 0).astype(F32)
    last = total[CHUNK - 1 :, :]
    leave = jnp.exp(last - total) * (pos >= first_last).astype(F32)
    through = jnp.exp(last) * (first_last < 0).astype(F32)
    return raw, dt, rate, total, bias, enter, leave, through


def shard_refs(refs, count):
    used = count + 1 if count == 4 else count
    return refs[:used], refs[used:]


def to_order(refs, buf, shift, count, at):
    for k in range(count):
        place = jnp.bitwise_xor(shift, k)
        if count == 4 and k == 3:
            low, high, blocks = refs[3], refs[4], at[1]

            @pl.when(at[0] < blocks // 2)
            def _():
                buf[place] = low[0]

            @pl.when(at[0] >= blocks // 2)
            def _():
                buf[place] = high[0]

        else:
            buf[place] = refs[k][0]


def shard_specs(count, blocks, q, width, place):
    one = pl.BlockSpec((1, q, width), lambda i, s: (place(i, s), 0, 0))
    if count != 4:
        return [one] * count
    half = blocks // 2
    low = pl.BlockSpec((1, q, width), lambda i, s: (jnp.minimum(place(i, s), half - 1), 0, 0))
    high = pl.BlockSpec((1, q, width), lambda i, s: (jnp.maximum(place(i, s) - half, 0), 0, 0))
    return [one, one, one, low, high]


QUARTERS = (((1, 3), (0, 2)), ((2, 3), (0, 1)))


def sum_shapes(count, blocks, q, width):
    if count != 4:
        return [jax.ShapeDtypeStruct((count, blocks, q, width), BF)]
    return [jax.ShapeDtypeStruct((2, blocks // 2, q, width), BF)] * 4


def sum_specs(count, blocks, q, width, step):
    if count != 4:
        return [pl.BlockSpec((count, 1, q, width), lambda i, s: (0, step(i) ^ s[1], 0, 0))]
    half = blocks // 2

    def lower(i, s):
        start = jnp.where(s[1] < half, 0, half)
        return (0, jnp.clip(step(i), start, start + half - 1) ^ s[1], 0, 0)

    def upper(i, s):
        start = jnp.where(s[1] < half, half, 0)
        return (0, (jnp.clip(step(i), start, start + half - 1) ^ s[1]) - half, 0, 0)

    return [pl.BlockSpec((2, 1, q, width), which) for which in (lower, lower, upper, upper)]


def sum_store(refs, buf, shift, at, blocks, count):
    if count != 4:
        for k in range(count):
            refs[0][k, 0] = buf[jnp.bitwise_xor(shift, k)]
        return
    for upper in range(2):

        @pl.when((at >= blocks // 2) == (upper == 1))
        def _():
            for which in range(2):
                for i, k in enumerate(QUARTERS[upper][which]):
                    refs[2 * upper + which][i, 0] = buf[jnp.bitwise_xor(shift, k)]


def conv_sum(ext, age, weights, bias_row, rows):
    out = jnp.zeros((rows, ext.shape[1]), F32) + bias_row
    for j in range(4):
        part = ext[pl.ds(HALO - j, rows), :]
        if j:
            part = jnp.where(age >= j, part, 0.0)
        out = out + weights[3 - j : 4 - j, :] * part
    return out


def forward_kernel(shift_ref, *refs, count, cd, ordered):
    unit_refs, refs = shard_refs(refs, count)
    weight_ref, age_ref, pc_ref, ph_ref, refs = *refs[:4], refs[4:]
    if not ordered:
        weight_out_ref, refs = refs[0], refs[1:]
    unit_ref, mixed_ref, gated_ref, pre_ref, ssd_ref, states_ref, refs = *refs[:6], refs[6:]
    if ordered:
        sums_ref, unit_buf, ext, state = refs
    else:
        used = 4 if count == 4 else 1
        sum_refs, (unit_buf, ext, state, gated_buf, sent_buf) = refs[:used], refs[used:]
    grid_at = pl.program_id(0)
    blocks = pl.num_programs(0)
    shift = shift_ref[0]
    conv_ch = cd + 2 * STATE
    q = unit_buf.shape[1]
    rows = count * q

    @pl.when(grid_at == 0)
    def _():
        ext[0:HALO, :] = jnp.zeros((HALO, conv_ch), F32)
        state[...] = jnp.zeros_like(state)

    @pl.when(grid_at > 0)
    def _():
        ext[0:HALO, :] = ext[rows : rows + HALO, :]

    to_order(unit_refs, unit_buf, shift, count, (jnp.bitwise_xor(grid_at, shift_ref[1]), blocks))
    unit = unit_buf[...].reshape(rows, unit_buf.shape[2])
    unit_ref[0] = unit
    mixed_ref[0] = mm(unit, weight_ref[...].reshape(-1, weight_ref.shape[2]))
    ext[HALO : HALO + rows, :] = mixed_ref[0, :, cd : cd + conv_ch]
    age = age_ref[0][:rows, :]
    pre = conv_sum(ext, age, pc_ref[0:4, :], pc_ref[4:5, :], rows)
    pre_ref[0] = pre
    xbc = (pre * jax.nn.sigmoid(pre)).astype(BF)
    skip_row = pc_ref[5:6, :cd]
    gain_row = pc_ref[6:7, :cd]
    bias_row = ph_ref[0:1, :]
    decay_row = ph_ref[1:2, :]
    spread = head_spread(cd)
    low_half = iota2((CHUNK, LANES), 1) < HEAD_DIM
    for c in range(rows // CHUNK):
        at = slice(c * CHUNK, (c + 1) * CHUNK)
        raw, dt, rate, total, bias, enter, leave, through = chunk_terms(
            mixed_ref[0, at, cd + conv_ch :], age[at], bias_row, decay_row
        )
        values = xbc[at, :cd]
        writers = xbc[at, cd : cd + STATE]
        readers = xbc[at, cd + STATE :]
        total_t = total.T
        dt_t = dt.T
        wide = mm_fine(
            jnp.concatenate([enter, leave * dt, jnp.broadcast_to(through, (8, LANES))], axis=0),
            spread,
            2,
        )
        scores = mm_bt(readers, writers)
        held = state[...]
        states_ref[0, c] = held.astype(BF)
        carried = mm(readers, held.astype(BF)) * wide[:CHUNK]
        values_f = values.astype(F32)
        pairs = []
        for pr in range(cd // LANES):
            mixing = []
            for h in (2 * pr, 2 * pr + 1):
                gap = total[:, h : h + 1] - total_t[h : h + 1, :] + bias
                mixing.append((jnp.exp(gap) * scores * dt_t[h : h + 1, :]).astype(BF))
            pair = values[:, pr * LANES : (pr + 1) * LANES]
            zero = jnp.zeros_like(pair)
            stacked = jnp.concatenate(
                [jnp.where(low_half, pair, zero), jnp.where(low_half, zero, pair)], axis=0
            )
            pairs.append(mm(jnp.concatenate(mixing, axis=1), stacked))
        ssd = jnp.concatenate(pairs, axis=1) + carried + skip_row * values_f
        ssd_ref[0, at, :] = ssd
        state[...] = held * wide[2 * CHUNK : 2 * CHUNK + 1] + mm_at(
            writers, (wide[CHUNK : 2 * CHUNK] * values_f).astype(BF)
        )
    ssd = ssd_ref[0]
    gate = mixed_ref[0, :, :cd]
    v = ssd * (gate * jax.nn.sigmoid(gate))
    squares = v * v
    partial_sums = squares[:, :LANES]
    for b in range(1, cd // LANES):
        partial_sums = partial_sums + squares[:, b * LANES : (b + 1) * LANES]
    weighted = v * gain_row
    gated = weighted.astype(BF).reshape(count, q, cd)
    sums = partial_sums.astype(BF).reshape(count, q, LANES)
    if ordered:
        gated_ref[:, 0] = gated
        sums_ref[:, 0] = sums
        return
    gated_buf[...] = gated
    for k in range(count):
        gated_ref[k, 0] = gated_buf[jnp.bitwise_xor(shift, k)]
    model = weight_out_ref.shape[1]
    product = mm(gated.reshape(rows, cd), weight_out_ref[...]).astype(BF)
    sent_buf[:, :, :model] = product.reshape(count, q, model)
    sent_buf[:, :, model:] = sums
    at = jnp.bitwise_xor(grid_at, shift_ref[1])
    sum_store(sum_refs, sent_buf, shift, at, blocks, count)


def backward_kernel(shift_ref, *refs, count, cd, own_scales):
    shift = shift_ref[0]
    grid_at = pl.program_id(0)
    blocks = pl.num_programs(0)
    if own_scales:
        grad_ref, scale_ref, refs = refs[0], refs[1], refs[2:]
    else:
        grad_refs, refs = shard_refs(refs, count)
        weight_out_ref, refs = refs[0], refs[1:]
    weight_ref, mixed_ref, age_ref, pc_ref, ph_ref, pre_ref, ssd_ref, states_ref = refs[:8]
    used = 4 if count == 4 else 1
    mixed_grad_ref, wide_sums, head_sums, sum_refs = *refs[8:11], refs[11 : 11 + used]
    out_buf, ext, adjoint, sent_buf = refs[11 + used : 15 + used]
    conv_ch = cd + 2 * STATE
    rows = mixed_ref.shape[1]
    q = rows // count

    @pl.when(grid_at == 0)
    def _():
        ext[rows : rows + HALO, :] = jnp.zeros((HALO, conv_ch), F32)
        adjoint[...] = jnp.zeros_like(adjoint)
        wide_sums[...] = jnp.zeros_like(wide_sums)
        head_sums[...] = jnp.zeros_like(head_sums)

    @pl.when(grid_at > 0)
    def _():
        ext[rows : rows + HALO, :] = ext[0:HALO, :]

    age_ext = age_ref[0]
    age = age_ext[:rows, :]
    skip_row = pc_ref[5:6, :cd]
    gain_row = pc_ref[6:7, :cd]
    bias_row = ph_ref[0:1, :]
    decay_row = ph_ref[1:2, :]

    if own_scales:
        extra = scale_ref[:, 0].reshape(rows, 2)
        scaled = grad_ref[:, 0].reshape(rows, cd) * extra[:, 0:1]
        mean_term = extra[:, 1:2]
    else:
        grad_buf = refs[15 + used]
        at = jnp.bitwise_xor(blocks - 1 - grid_at, shift_ref[1])
        to_order(grad_refs, grad_buf, shift, count, (at, blocks))
        grad = grad_buf[...].reshape(rows, grad_buf.shape[2])
        model = weight_out_ref.shape[1]
        scaled = mm_bt(grad[:, :model], weight_out_ref[...])
        extra = grad[:, model:].astype(F32)
        mean_term = extra[:, 0:1] + extra[:, 1:2]
    gate = mixed_ref[0, :, :cd]
    ssd = ssd_ref[0]
    sg = jax.nn.sigmoid(gate)
    sl = gate * sg
    v = ssd * sl
    v_grad = scaled * gain_row - mean_term * v
    wide_sums[6:7, :cd] += jnp.sum(scaled * v, axis=0, keepdims=True)
    d_ssd = v_grad * sl
    d_gate = v_grad * ssd * (sg * (1.0 + gate * (1.0 - sg)))
    out_buf[:, :cd] = d_gate.astype(BF)

    pre = pre_ref[0]
    sp = jax.nn.sigmoid(pre)
    xbc = (pre * sp).astype(BF)
    d_silu = sp * (1.0 + pre * (1.0 - sp))
    spread = head_spread(cd)
    gather = head_gather(cd)
    low_half = iota2((CHUNK, LANES), 1) < HEAD_DIM
    tri_rows = iota2((CHUNK, CHUNK), 0)
    tri_cols = iota2((CHUNK, CHUNK), 1)
    from_here = (tri_cols >= tri_rows).astype(BF)
    before = (tri_cols < tri_rows).astype(BF)
    heads = cd // HEAD_DIM
    pick_shape = (heads * CHUNK, LANES)
    pick_head = (iota2(pick_shape, 0) // CHUNK == iota2(pick_shape, 1)).astype(BF)

    for c in reversed(range(rows // CHUNK)):
        at = slice(c * CHUNK, (c + 1) * CHUNK)
        raw, dt, rate, total, bias, enter, leave, through = chunk_terms(
            mixed_ref[0, at, cd + conv_ch :], age[at], bias_row, decay_row
        )
        values = xbc[at, :cd]
        writers = xbc[at, cd : cd + STATE]
        readers = xbc[at, cd + STATE :]
        values_f = values.astype(F32)
        dy = d_ssd[at]
        wide_sums[5:6, :cd] += jnp.sum(values_f * dy, axis=0, keepdims=True)
        total_t = total.T
        dt_t = dt.T
        wide = mm_fine(
            jnp.concatenate([enter, leave, dt, jnp.broadcast_to(through, (8, LANES))], axis=0),
            spread,
            2,
        )
        enter_w = wide[:CHUNK]
        leave_w = wide[CHUNK : 2 * CHUNK]
        dt_w = wide[2 * CHUNK : 3 * CHUNK]
        through_w = wide[3 * CHUNK : 3 * CHUNK + 1]
        held = states_ref[0, c]
        adj = adjoint[...]
        adj_b = adj.astype(BF)
        scores = mm_bt(readers, writers)
        entered = enter_w * dy
        entered_b = entered.astype(BF)
        row_enter = entered * mm(readers, held)
        d_readers = mm_bt(entered_b, held)
        from_state = leave_w * mm(writers, adj_b)
        exits = values_f * from_state * dt_w
        d_writers = mm_bt((leave_w * dt_w * values_f).astype(BF), adj_b)
        through_sum = jnp.sum(adj * held.astype(F32), axis=0, keepdims=True) * through_w
        adjoint[...] = adj * through_w + mm_at(readers, entered_b)
        d_scores = jnp.zeros((CHUNK, CHUNK), F32)
        pulls = []
        kernels = []
        for pr in range(cd // LANES):
            dy_pair = dy[:, pr * LANES : (pr + 1) * LANES].astype(BF)
            zero = jnp.zeros_like(dy_pair)
            stacked = jnp.concatenate(
                [jnp.where(low_half, dy_pair, zero), jnp.where(low_half, zero, dy_pair)], axis=0
            )
            d_mix = mm_bt(stacked, values[:, pr * LANES : (pr + 1) * LANES])
            mixing = []
            for i, h in enumerate((2 * pr, 2 * pr + 1)):
                gap = total[:, h : h + 1] - total_t[h : h + 1, :] + bias
                decays = jnp.exp(gap)
                mixing.append((decays * scores).astype(BF))
                pull = d_mix[i * CHUNK : (i + 1) * CHUNK] * dt_t[h : h + 1, :] * decays
                d_scores = d_scores + pull
                kernels.append((pull * scores).astype(BF))
            pulls.append(mm_at(jnp.concatenate(mixing, axis=0), stacked))
        d_scaled = jnp.concatenate(pulls, axis=1) + from_state
        per_head = mm_fine(
            jnp.concatenate(
                [row_enter, exits, values_f * d_scaled, jnp.broadcast_to(through_sum, (8, cd))],
                axis=0,
            ),
            gather,
            2,
        )
        row_enter = per_head[:CHUNK]
        exits = per_head[CHUNK : 2 * CHUNK]
        d_dt = per_head[2 * CHUNK : 3 * CHUNK]
        passing = per_head[3 * CHUNK : 3 * CHUNK + 1]
        row_sums = mm(jnp.concatenate(kernels, axis=1), pick_head)
        col_sums = mm_at(jnp.concatenate(kernels, axis=0), pick_head)
        d_rate = (
            mm_fine_right(from_here, row_sums - col_sums + row_enter, 3)
            + mm_fine_right(before, exits, 3)
            + passing
        )
        d_raw = (d_dt - d_rate * decay_row) * jax.nn.sigmoid(raw)
        head_sums[0:1, :] += jnp.sum(d_raw, axis=0, keepdims=True)
        head_sums[1:2, :] += jnp.sum(d_rate * rate, axis=0, keepdims=True)
        d_scores_b = d_scores.astype(BF)
        d_readers = d_readers + mm(d_scores_b, writers)
        d_writers = d_writers + mm_at(d_scores_b, readers)
        d_values = dt_w * d_scaled + skip_row * dy
        ext[at, :] = jnp.concatenate([d_values, d_writers, d_readers], axis=1) * d_silu[at]
        out_buf[at, cd + conv_ch :] = d_raw.astype(BF)
    conv_in = mixed_ref[0, :, cd : cd + conv_ch]
    d_conv = jnp.zeros((rows, conv_ch), F32)
    for j in range(4):
        part = ext[pl.ds(j, rows), :]
        if j:
            part = jnp.where(age_ext[j : j + rows, :] >= j, part, 0.0)
        else:
            wide_sums[4:5, :] += jnp.sum(part, axis=0, keepdims=True)
        d_conv = d_conv + pc_ref[3 - j : 4 - j, :] * part
        wide_sums[3 - j : 4 - j, :] += jnp.sum(part * conv_in, axis=0, keepdims=True)
    out_buf[:, cd : cd + conv_ch] = d_conv.astype(BF)
    mixed_grad_ref[0] = out_buf[...]
    weight = weight_ref[...].reshape(-1, weight_ref.shape[2])
    unit_grad = mm_bt(out_buf[...], weight).astype(BF)
    sent_buf[...] = unit_grad.reshape(sent_buf.shape)
    at = jnp.bitwise_xor(blocks - 1 - grid_at, shift_ref[1])
    sum_store(sum_refs, sent_buf, shift, at, blocks, count)


def whole(shape):
    return pl.BlockSpec(shape, lambda *_: (0,) * len(shape), pipeline_mode=pl.Buffered(1))


def mixer_forward(shift, units, weight, weight_out, age, pc, ph):
    count = len(units)
    blocks, q, model = units[0].shape
    width = weight.shape[2]
    weight_block = (weight.shape[0], model // weight.shape[0], width)
    conv_ch = pc.shape[1]
    cd = conv_ch - 2 * STATE
    rows = count * q
    chunks = rows // CHUNK
    in_specs = shard_specs(count, blocks, q, model, lambda i, s: i ^ s[1]) + [
        whole(weight_block),
        pl.BlockSpec((1, rows + HALO, 1), lambda i, s: (i, 0, 0)),
        whole(pc.shape),
        whole(ph.shape),
    ]
    ordered = weight_out is None
    args = flat_shards(units) + [weight, age, pc, ph]
    if not ordered:
        in_specs.append(whole(weight_out.shape))
        args.append(weight_out)

    def in_order(*shape):
        return pl.BlockSpec((1,) + shape, lambda i, s: (i,) + (0,) * len(shape))

    def relative(last):
        return pl.BlockSpec((count, 1, q, last), lambda i, s: (0, i ^ s[1], 0, 0))

    scratch = [
        pltpu.VMEM((count, q, model), BF),
        pltpu.VMEM((rows + HALO, conv_ch), F32),
        pltpu.VMEM((STATE, cd), F32),
    ]
    if ordered:
        last_shapes = [jax.ShapeDtypeStruct((count, blocks, q, LANES), BF)]
        last_specs = [relative(LANES)]
    else:
        last_shapes = sum_shapes(count, blocks, q, model + LANES)
        last_specs = sum_specs(count, blocks, q, model + LANES, lambda i: i)
        scratch += [
            pltpu.VMEM((count, q, cd), BF),
            pltpu.VMEM((count, q, model + LANES), BF),
        ]
    return pl.pallas_call(
        partial(forward_kernel, count=count, cd=cd, ordered=ordered),
        out_shape=[
            jax.ShapeDtypeStruct((blocks, rows, model), BF),
            jax.ShapeDtypeStruct((blocks, rows, width), F32),
            jax.ShapeDtypeStruct((count, blocks, q, cd), BF),
            jax.ShapeDtypeStruct((blocks, rows, conv_ch), F32),
            jax.ShapeDtypeStruct((blocks, rows, cd), F32),
            jax.ShapeDtypeStruct((blocks, chunks, STATE, cd), BF),
        ]
        + last_shapes,
        grid_spec=pltpu.PrefetchScalarGridSpec(
            num_scalar_prefetch=1,
            grid=(blocks,),
            in_specs=in_specs,
            out_specs=[
                in_order(rows, model),
                in_order(rows, width),
                relative(cd),
                in_order(rows, conv_ch),
                in_order(rows, cd),
                in_order(chunks, STATE, cd),
            ]
            + last_specs,
            scratch_shapes=scratch,
        ),
        compiler_params=pltpu.CompilerParams(vmem_limit_bytes=52 * 2**20),
        cost_estimate=pl.CostEstimate(flops=10**6, bytes_accessed=10**5, transcendentals=0),
    )(shift, *args)


def flat_shards(shards):
    out = []
    for shard in shards:
        out += list(shard) if isinstance(shard, tuple) else [shard]
    return out


def mixer_backward(
    shift, grads, scales, weight_out, weight, mixed, age, pc, ph, pre, ssd, states, model
):
    blocks, rows, width = mixed.shape
    weight_block = (weight.shape[0], model // weight.shape[0], width)
    conv_ch = pc.shape[1]
    cd = conv_ch - 2 * STATE
    chunks = rows // CHUNK
    top = blocks - 1
    if scales is not None:
        count, _, q, _ = grads.shape
        in_specs = [
            pl.BlockSpec((count, 1, q, cd), lambda i, s: (0, (top - i) ^ s[1], 0, 0)),
            pl.BlockSpec((count, 1, q, 2), lambda i, s: (0, (top - i) ^ s[1], 0, 0)),
        ]
        args = [grads, scales]
    else:
        count = len(grads)
        _, q, grad_width = grads[0].shape
        in_specs = shard_specs(count, blocks, q, grad_width, lambda i, s: (top - i) ^ s[1])
        in_specs.append(whole(weight_out.shape))
        args = flat_shards(grads) + [weight_out]

    def in_order(*shape):
        return pl.BlockSpec((1,) + shape, lambda i, s: (top - i,) + (0,) * len(shape))

    in_specs += [
        whole(weight_block),
        in_order(rows, width),
        in_order(rows + HALO, 1),
        whole(pc.shape),
        whole(ph.shape),
        in_order(rows, conv_ch),
        in_order(rows, cd),
        in_order(chunks, STATE, cd),
    ]
    args += [weight, mixed, age, pc, ph, pre, ssd, states]
    scratch = [
        pltpu.VMEM((rows, width), BF),
        pltpu.VMEM((rows + HALO, conv_ch), F32),
        pltpu.VMEM((STATE, cd), F32),
        pltpu.VMEM((count, q, model), BF),
    ]
    if scales is None:
        scratch.append(pltpu.VMEM((count, q, grad_width), BF))
    return pl.pallas_call(
        partial(backward_kernel, count=count, cd=cd, own_scales=scales is not None),
        out_shape=[
            jax.ShapeDtypeStruct((blocks, rows, width), BF),
            jax.ShapeDtypeStruct((8, conv_ch), F32),
            jax.ShapeDtypeStruct((8, LANES), F32),
        ]
        + sum_shapes(count, blocks, q, model),
        grid_spec=pltpu.PrefetchScalarGridSpec(
            num_scalar_prefetch=1,
            grid=(blocks,),
            in_specs=in_specs,
            out_specs=[
                in_order(rows, width),
                pl.BlockSpec((8, conv_ch), lambda i, s: (0, 0)),
                pl.BlockSpec((8, LANES), lambda i, s: (0, 0)),
            ]
            + sum_specs(count, blocks, q, model, lambda i: top - i),
            scratch_shapes=scratch,
        ),
        compiler_params=pltpu.CompilerParams(vmem_limit_bytes=52 * 2**20),
        cost_estimate=pl.CostEstimate(
            flops=4 * 10**10, bytes_accessed=5 * 10**7, transcendentals=2 * 10**6
        ),
    )(shift, *args)


SMALL_ROWS = 16


def shard_kernel(at_ref, *refs, cd, hd, small):
    gate_ref, values_ref, rest_ref, step_ref, gain_ref, refs = *refs[:5], refs[5:]
    gain = gain_ref[...]
    rows = gain.shape[0]
    conv_ch = cd + 2 * STATE

    def scaled(ref):
        return (ref[0].astype(F32) * gain).astype(BF)

    out_ref = refs[small]
    out_ref[0:rows, :cd] = scaled(gate_ref)
    out_ref[0:rows, cd : 2 * cd] = scaled(values_ref)
    out_ref[0:rows, 2 * cd : cd + conv_ch] = scaled(rest_ref)
    steps = step_ref[0]
    shape = (steps.shape[0], LANES)
    heads, cols = iota2(shape, 0), iota2(shape, 1)
    chosen = ((heads == at_ref[0] * hd + cols) & (cols < hd)).astype(BF)
    out_ref[0:rows, cd + conv_ch :] = (mm_at(steps, chosen) * gain).astype(BF)
    if small:
        buf = refs[small + 1]
        buf[...] = jnp.zeros_like(buf)
        at, lane = 0, 0
        for ref in refs[:small]:
            count, lanes = ref.shape
            buf[at : at + count, lane : lane + lanes] = ref[...].astype(F32)
            if lanes < LANES:
                lane += LANES
            else:
                at += count
        out_ref[rows : rows + SMALL_ROWS, :] = buf[...].astype(BF)


def weight_shard(shift, layer, input_proj, step_proj, gain, cd, hd, small=()):
    _, rows, columns = input_proj.shape
    heads = step_proj.shape[1]
    parts = heads // hd
    at_rest = (columns - 2 * STATE) // (2 * STATE)
    width = 2 * cd + 2 * STATE + LANES
    full = rows + SMALL_ROWS if small else rows
    return pl.pallas_call(
        partial(shard_kernel, cd=cd, hd=hd, small=len(small)),
        out_shape=jax.ShapeDtypeStruct((full, width), BF),
        grid_spec=pltpu.PrefetchScalarGridSpec(
            num_scalar_prefetch=1,
            grid=(1,),
            in_specs=[
                pl.BlockSpec((1, rows, cd), lambda i, s: (layer, 0, s[0])),
                pl.BlockSpec((1, rows, cd), lambda i, s: (layer, 0, parts + s[0])),
                pl.BlockSpec((1, rows, 2 * STATE), lambda i, s: (layer, 0, at_rest)),
                pl.BlockSpec((1, heads, rows), lambda i, s: (layer, 0, 0)),
                whole((rows, 1)),
            ]
            + [whole(x.shape) for x in small],
            out_specs=pl.BlockSpec((full, width), lambda i, s: (0, 0)),
            scratch_shapes=[pltpu.VMEM((SMALL_ROWS, width), F32)] if small else [],
        ),
        compiler_params=pltpu.CompilerParams(vmem_limit_bytes=40 * 2**20),
        cost_estimate=pl.CostEstimate(flops=10**6, bytes_accessed=10**5, transcendentals=0),
    )(shift, input_proj, input_proj, input_proj, step_proj, gain[:, None], *small)


def place_kernel(shift_ref, *refs, count, dim):
    out_ref = refs[count]
    for k in range(count):
        at = (slice(None),) * dim + (jnp.bitwise_xor(shift_ref[0], k),)
        out_ref[at] = refs[k][...]


def place(shift, parts, dim):
    shape = parts[0].shape
    full = shape[:dim] + (len(parts),) + shape[dim:]
    return pl.pallas_call(
        partial(place_kernel, count=len(parts), dim=dim),
        out_shape=jax.ShapeDtypeStruct(full, parts[0].dtype),
        grid_spec=pltpu.PrefetchScalarGridSpec(
            num_scalar_prefetch=1,
            grid=(1,),
            in_specs=[whole(part.shape) for part in parts],
            out_specs=whole(full),
        ),
        compiler_params=pltpu.CompilerParams(vmem_limit_bytes=40 * 2**20),
        cost_estimate=pl.CostEstimate(flops=10**6, bytes_accessed=10**5, transcendentals=0),
    )(shift, *parts)


def term_specs(terms, q):
    specs, kinds = [], []
    for array, kind in terms:
        lead = array.ndim - 3
        blocks, width = array.shape[lead], array.shape[-1]
        half = blocks // 2 if kind == "all" else blocks

        def place(i, lead=lead, kind=kind):
            return (0,) * lead + (i if kind == "all" else 0, 0, 0)

        specs.append(pl.BlockSpec((1,) * lead + (half, q, width), place))
        kinds.append(kind)
    return specs, kinds


def add_terms(refs, kinds, buf):
    at = pl.program_id(0)

    def total(kind):
        out = None
        for ref, own in zip(refs, kinds):
            if own == kind:
                part = ref[...].reshape(buf.shape).astype(F32)
                out = part if out is None else out + part
        return out

    if "all" in kinds:
        buf[...] = total("all")
        return

    @pl.when(at == 0)
    def _():
        buf[...] = total("lower")

    @pl.when(at == 1)
    def _():
        buf[...] = total("upper")


def settle_forward_kernel(*refs, kinds, inner):
    term_refs, refs = refs[: len(kinds)], refs[len(kinds) :]
    resid_ref, out_ref, branch_ref, ginv_ref, inv_ref, unit_ref, buf = refs
    add_terms(term_refs, kinds, buf)
    model = resid_ref.shape[2]
    squares = jnp.sum(buf[:, model:], axis=1, keepdims=True)
    ginv = lax.rsqrt(squares / inner + EPSILON)
    branch = buf[:, :model] * ginv
    resid = resid_ref[...].reshape(branch.shape) + branch
    inv = lax.rsqrt(jnp.mean(resid * resid, axis=1, keepdims=True) + EPSILON)
    out_ref[...] = resid.reshape(out_ref.shape)
    branch_ref[...] = branch.reshape(branch_ref.shape)
    ginv_ref[...] = ginv.reshape(ginv_ref.shape)
    inv_ref[...] = inv.reshape(inv_ref.shape)
    unit_ref[...] = (resid * inv).astype(BF).reshape(unit_ref.shape)


def settle_forward(terms, resid, inner):
    blocks, q, model = resid.shape
    specs, kinds = term_specs(terms, q)
    half = blocks // 2
    wide = pl.BlockSpec((half, q, model), lambda i: (i, 0, 0))
    thin = pl.BlockSpec((half, q, 1), lambda i: (i, 0, 0))
    return pl.pallas_call(
        partial(settle_forward_kernel, kinds=kinds, inner=inner),
        grid=(2,),
        out_shape=[
            jax.ShapeDtypeStruct(resid.shape, F32),
            jax.ShapeDtypeStruct(resid.shape, F32),
            jax.ShapeDtypeStruct((blocks, q, 1), F32),
            jax.ShapeDtypeStruct((blocks, q, 1), F32),
            jax.ShapeDtypeStruct(resid.shape, BF),
        ],
        in_specs=specs + [wide],
        out_specs=[wide, wide, thin, thin, wide],
        compiler_params=pltpu.CompilerParams(vmem_limit_bytes=40 * 2**20),
        scratch_shapes=[pltpu.VMEM((half * q, terms[0][0].shape[-1]), F32)],
        cost_estimate=pl.CostEstimate(flops=10**6, bytes_accessed=10**5, transcendentals=0),
    )(*[array for array, _ in terms], resid)


def settle_backward_kernel(*refs, kinds, inner, onward):
    term_refs, refs = refs[: len(kinds)], refs[len(kinds) :]
    resid_ref, inv_ref, back_ref, refs = refs[0], refs[1], refs[2], refs[3:]
    buf = refs[-1]
    add_terms(term_refs, kinds, buf)
    grad = buf[...]
    inv = inv_ref[...].reshape(grad.shape[0], 1)
    u = resid_ref[...].reshape(grad.shape) * inv
    back = back_ref[...].astype(F32).reshape(grad.shape) + inv * (
        grad - u * jnp.mean(grad * u, axis=1, keepdims=True)
    )
    if not onward:
        refs[0][...] = back.astype(BF).reshape(refs[0].shape)
        return
    branch_ref, ginv_ref, out_ref, payload_ref = refs[:4]
    out_ref[...] = back.reshape(out_ref.shape)
    model = back.shape[1]
    low = back.astype(BF).astype(F32)
    ginv = ginv_ref[...].reshape(inv.shape)
    mean = jnp.sum(low * branch_ref[...].reshape(low.shape), axis=1, keepdims=True) / inner
    kappa = ginv * ginv * mean
    high = kappa.astype(BF).astype(F32)
    lane = iota2((back.shape[0], LANES), 1)
    front = payload_ref.shape[:2]
    payload_ref[:, :, :model] = (low * ginv).astype(BF).reshape(*front, model)
    tail = jnp.where(lane == 0, high, jnp.where(lane == 1, kappa - high, 0.0))
    payload_ref[:, :, model:] = tail.astype(BF).reshape(*front, LANES)


def settle_backward(terms, resid, inv, back, inner, branch=None, ginv=None):
    blocks, q, model = resid.shape
    specs, kinds = term_specs(terms, q)
    onward = branch is not None
    half = blocks // 2
    wide = pl.BlockSpec((half, q, model), lambda i: (i, 0, 0))
    thin = pl.BlockSpec((half, q, 1), lambda i: (i, 0, 0))
    args = [array for array, _ in terms] + [resid, inv, back]
    in_specs = specs + [wide, thin, wide]
    if onward:
        args += [branch, ginv]
        in_specs += [wide, thin]
        out_shape = [
            jax.ShapeDtypeStruct(resid.shape, F32),
            jax.ShapeDtypeStruct((blocks, q, model + LANES), BF),
        ]
        out_specs = [wide, pl.BlockSpec((half, q, model + LANES), lambda i: (i, 0, 0))]
    else:
        out_shape = [jax.ShapeDtypeStruct(resid.shape, BF)]
        out_specs = [wide]
    limit = 40 if onward else 60
    return pl.pallas_call(
        partial(settle_backward_kernel, kinds=kinds, inner=inner, onward=onward),
        grid=(2,),
        out_shape=out_shape,
        in_specs=in_specs,
        out_specs=out_specs,
        compiler_params=pltpu.CompilerParams(vmem_limit_bytes=limit * 2**20),
        scratch_shapes=[pltpu.VMEM((half * q, model), F32)],
        cost_estimate=pl.CostEstimate(flops=10**6, bytes_accessed=10**5, transcendentals=0),
    )(*args)


def finish_kernel(shift_ref, *refs, count, cd, hd, inner, rows, out_part, apart):
    part_refs, refs = refs[:count], refs[count:]
    own_refs, refs = (refs[:count], refs[count:]) if apart else (None, refs)
    weight_ref, step_ref, gain_ref, gain_row_ref = refs[:4]
    grad_ref, out_ref, steps_ref, norm_ref, norm_row_ref = refs[-5:]
    gain = gain_ref[...]
    norm = jnp.zeros((rows, 1), F32)

    def put(at, value, norm):
        cols = pl.ds(at, value.shape[1])
        grad_ref[0, :, cols] = value * gain
        return norm + jnp.sum(
            value * weight_ref[0, :, cols].astype(F32), axis=1, keepdims=True
        )

    rest = jnp.zeros((rows, 2 * STATE), F32)
    heads = step_ref.shape[1]
    steps = jnp.zeros((heads, rows), F32)
    head, lane = iota2((heads, LANES), 0), iota2((heads, LANES), 1)
    for k in range(count):
        j = jnp.bitwise_xor(shift_ref[0], k)
        part = part_refs[k][:rows, :]
        chosen = ((head == j * hd + lane) & (lane < hd)).astype(BF)
        steps = steps + mm_bt(chosen, part[:, 2 * cd + 2 * STATE :])
        part = part.astype(F32)
        norm = put(pl.multiple_of(j * cd, LANES), part[:, :cd], norm)
        norm = put(pl.multiple_of(inner + j * cd, LANES), part[:, cd : 2 * cd], norm)
        rest = rest + part[:, 2 * cd : 2 * cd + 2 * STATE]
        own = (own_refs[k][...] if apart else part_refs[k][rows:, :]).astype(F32)
        out_ref[0, pl.ds(pl.multiple_of(j * out_part, 8), out_part), :] = own[
            :out_part, : out_ref.shape[2]
        ]
    norm_ref[...] = put(2 * inner, rest, norm)
    norm_row_ref[...] = jnp.sum(steps * step_ref[0].astype(F32), axis=0, keepdims=True)
    steps_ref[0] = steps * gain_row_ref[...]


def finish(layer, shift, parts, apart, weight, step, gain, out_part, out_cols, before, cd, inner):
    count = len(parts)
    layers, rows, columns = weight.shape
    heads = step.shape[1]
    in_specs = [whole(part.shape) for part in parts + (apart or [])] + [
        pl.BlockSpec((1, rows, columns), lambda i, s: (layer, 0, 0)),
        pl.BlockSpec((1, heads, rows), lambda i, s: (layer, 0, 0)),
        whole((rows, 1)),
        whole((1, rows)),
    ]
    args = parts + (apart or []) + [weight, step, gain[:, None], gain[None, :]]
    aliases = {}
    if before is not None:
        aliases = {len(args) + 1 + i: i for i in range(3)}
        in_specs += [pl.BlockSpec(memory_space=pl.ANY)] * 3
        args += list(before)
    return pl.pallas_call(
        partial(
            finish_kernel,
            count=count,
            cd=cd,
            hd=heads // count,
            inner=inner,
            rows=rows,
            out_part=out_part,
            apart=apart is not None,
        ),
        out_shape=[
            jax.ShapeDtypeStruct((layers, rows, columns), F32),
            jax.ShapeDtypeStruct((layers, count * out_part, out_cols), F32),
            jax.ShapeDtypeStruct((layers, heads, rows), F32),
            jax.ShapeDtypeStruct((rows, 1), F32),
            jax.ShapeDtypeStruct((1, rows), F32),
        ],
        grid_spec=pltpu.PrefetchScalarGridSpec(
            num_scalar_prefetch=1,
            grid=(1,),
            in_specs=in_specs,
            out_specs=[
                pl.BlockSpec((1, rows, columns), lambda i, s: (layer, 0, 0)),
                pl.BlockSpec((1, count * out_part, out_cols), lambda i, s: (layer, 0, 0)),
                pl.BlockSpec((1, heads, rows), lambda i, s: (layer, 0, 0)),
                whole((rows, 1)),
                whole((1, rows)),
            ],
        ),
        input_output_aliases=aliases,
        compiler_params=pltpu.CompilerParams(vmem_limit_bytes=40 * 2**20),
        cost_estimate=pl.CostEstimate(flops=10**6, bytes_accessed=10**5, transcendentals=0),
    )(shift, *args)


def swap(value, axis, k, size):
    return lax.ppermute(value, axis, [(i, i ^ k) for i in range(size)])


def pick(value, index):
    return lax.dynamic_index_in_dim(value, index, 0, keepdims=False)


def tie(*values):
    return lax.optimization_barrier(values)


def after(value, *first):
    return lax.optimization_barrier((value, first))[0]


def sends(parts, base, size):
    return [pick(parts, base ^ k) for k in range(size)]


def moved(items, axis, what):
    size = len(items)
    with jax.named_scope(what):
        return [items[0]] + [swap(items[k], axis, k, size) for k in range(1, size)]


def gather_first(shard, n, what):
    if n != 4:
        return [lax.all_gather(shard, "dp")]
    with jax.named_scope(what):
        return [shard, swap(shard, "dp", 1, n), swap(shard, "dp", 2, n)]


def gather_second(state, n, what):
    if n != 4:
        mine = lax.axis_index("dp")
        return [pick(state[0], mine ^ k) for k in range(n)]
    shard, first, second = state
    half = shard.shape[0] // 2
    with jax.named_scope(what):
        low = swap(first[:half], "dp", 2, n)
        high = swap(second[half:], "dp", 1, n)
    return [shard, first, second, (low, high)]


def tie_terms(terms, rest):
    arrays, rest = tie([array for array, _ in terms], rest)
    return [(array, kind) for array, (_, kind) in zip(arrays, terms)], rest


def joined(shards):
    return [
        jnp.concatenate(shard, axis=0) if isinstance(shard, tuple) else shard for shard in shards
    ]


def reduce_first(parts, n, what):
    if n != 4:
        mine = lax.axis_index("dp")
        ordered = jnp.stack([pick(parts[0], mine ^ j) for j in range(n)])
        return [lax.psum_scatter(ordered, "dp", scatter_dimension=0, tiled=False)]
    send_a, keep_a, send_b, keep_b = parts
    with jax.named_scope(what):
        return [keep_a, keep_b, swap(send_a, "dp", 1, n), swap(send_b, "dp", 2, n)]


def reduce_second(state, n, what):
    if n != 4:
        return [(state[0], "all")]
    keep_a, keep_b, got_a, got_b = state
    with jax.named_scope(what):
        on_a = (keep_a[1].astype(F32) + got_a[1].astype(F32)).astype(BF)
        on_b = (keep_b[1].astype(F32) + got_b[1].astype(F32)).astype(BF)
        last_a = swap(on_a, "dp", 2, n)
        last_b = swap(on_b, "dp", 1, n)
    lower = [(x, "lower") for x in (keep_a, got_a, last_a)]
    return lower + [(x, "upper") for x in (keep_b, got_b, last_b)]


def split_sums(parts, n):
    if n != 4:
        return [parts]
    half = parts.shape[1] // 2
    out = []
    for upper in range(2):
        side = parts[:, upper * half : (upper + 1) * half]
        out += [jnp.stack([side[k] for k in pair]) for pair in QUARTERS[upper]]
    return out


def add_up(terms):
    sums = {}
    for array, kind in terms:
        part = (array if array.ndim == 3 else array[0]).astype(F32)
        sums[kind] = part if kind not in sums else sums[kind] + part
    if "all" in sums:
        return sums["all"]
    return jnp.concatenate([sums["lower"], sums["upper"]], axis=0)


def both_cores(block, what):
    core = lax.axis_index("core")
    keep = pick(block, core)
    with jax.named_scope(what):
        other = lax.ppermute(pick(block, 1 - core), "core", [(0, 1), (1, 0)])
    first = jnp.where(core == 0, keep, other)
    second = jnp.where(core == 0, other, keep)
    return jnp.concatenate([first, second], axis=0)


def to_groups(both, n, what):
    q = both.shape[0] // n
    d = lax.axis_index("dp")
    return jnp.stack(moved(sends(both.reshape(n, q, -1), d, n), "dp", what))


def to_chunks(groups, z_count, what):
    d, z = lax.axis_index("dp"), lax.axis_index("z")
    return jnp.stack(moved(sends(groups, z ^ d, z_count), "z", what))


def from_both(groups, q, what):
    n = len(groups)
    d, core = lax.axis_index("dp"), lax.axis_index("core")
    half = n // 2
    parts = jnp.stack([group[:q] for group in groups])
    sums = jnp.stack([group[q:] for group in groups])

    def side(c):
        return jnp.concatenate([pick(parts, (half * c + i) ^ d) for i in range(half)], axis=0)

    with jax.named_scope(what):
        other, more = lax.ppermute((side(1 - core), sums), "core", [(0, 1), (1, 0)])
    keep = side(core)
    sums = sums.astype(F32) + more.astype(F32)
    both = jnp.stack([jnp.where(core == 0, keep, other), jnp.where(core == 0, other, keep)])
    return both, [pick(sums, d ^ j) for j in range(n)]


def on_device(
    hidden_in,
    doc_lengths,
    norm_gain,
    input_proj,
    step_proj,
    conv_weight,
    conv_bias,
    step_bias,
    decay_log,
    skip_gain,
    gate_gain,
    output_proj,
    cotangent,
    *,
    n,
    z_count,
):
    layers = norm_gain.shape[0]
    owners = 2 * z_count
    d_rows = norm_gain.shape[1]
    width_d = d_rows * owners
    heads_f = step_bias.shape[1]
    heads = heads_f * owners
    hd = heads // n
    cd = hd * HEAD_DIM
    inner = heads * HEAD_DIM
    conv_f = conv_bias.shape[1]
    conv_ch = cd + 2 * STATE
    gate_f = gate_gain.shape[1]
    out_rows = output_proj.shape[1]
    width_in = cd + conv_ch + LANES
    step_at = cd + conv_ch
    d = lax.axis_index("dp")
    z = lax.axis_index("z")
    core = lax.axis_index("core")
    shift = jnp.stack([d, z]).astype(jnp.int32)

    small_lanes = max(-(-max(conv_f, gate_f) // LANES), 3) * LANES

    def small_unpack(everything):
        everything = everything.astype(F32)

        def rows(at, count, lanes):
            part = everything[:, at : at + count, lanes]
            return part.transpose(1, 0, 2).reshape(count, -1)

        def mine(x):
            width = x.shape[1] // n
            return lax.dynamic_slice_in_dim(x, d * width, width, 1)

        conv = rows(0, 5 * layers, slice(0, conv_f))
        conv = jnp.concatenate([mine(conv[:, :inner]), conv[:, inner:]], axis=1)
        gain = mine(rows(5 * layers, layers, slice(0, gate_f)))
        at = 6 * layers
        bias, decay, skip = (
            mine(rows(at, layers, slice(i * LANES, i * LANES + heads_f))) for i in range(3)
        )
        skip = jnp.broadcast_to(skip[:, :, None], (layers, hd, HEAD_DIM)).reshape(layers, cd)
        wide = jnp.pad(jnp.stack([skip, gain], axis=1), ((0, 0), (0, 1), (0, 2 * STATE)))
        head = jnp.stack([bias, jnp.exp(decay)], axis=1)
        head = jnp.pad(head, ((0, 0), (0, 6), (0, LANES - hd)))
        pcs = [
            jnp.concatenate(
                [conv[4 * l : 4 * l + 4], conv[4 * layers + l : 4 * layers + l + 1], wide[l]],
                axis=0,
            )
            for l in range(layers)
        ]
        return pcs, [head[l] for l in range(layers)]

    out_part = out_rows // n

    def shard_out(layer):
        return lax.dynamic_slice_in_dim(output_proj[layer], d * out_part, out_part, 0)

    def column_sends(column):
        return sends(column.reshape(n, 2, out_part, width_d), d, n)

    def weight_out(parts):
        return place(shift, parts, 1).reshape(cd, width_d)

    every = ("dp", "z", "core")

    def at_device(i, j, c):
        return (i * z_count + j) * 2 + c

    both_ways = [
        (at_device(i, g // 2, g % 2), at_device(g % n, i, g // n))
        for i in range(n)
        for g in range(2 * n)
    ]

    def to_slices(own, what):
        with jax.named_scope(what):
            return lax.ppermute(own, every, [(b, a) for a, b in both_ways])

    def to_owners(piece, what):
        with jax.named_scope(what):
            return lax.ppermute(piece, every, both_ways)

    def grad_out_sum(d_out):
        pieces = d_out.reshape(owners, out_part, width_d)
        return lax.psum_scatter(pieces, PLANE, scatter_dimension=0)

    def grad_out_sends(d_out):
        return sends(d_out.reshape(2, n, out_part, width_d).transpose(1, 0, 2, 3), d, n)

    def grad_out_owned(by_rows):
        rows_all = place(shift, by_rows, 0).reshape(owners, out_part, width_d)
        return lax.psum_scatter(rows_all, PLANE, scatter_dimension=0)

    def grad_in(unit_cat, d_mixed):
        return mm_at(flat(unit_cat), flat(d_mixed)).astype(BF)

    out_padded = -(-out_part // 16) * 16

    def owned_first(own_in, own_out, what):
        own_out = jnp.pad(own_out, ((0, out_padded - out_part), (0, 0)))
        if n != 4:
            return tuple(
                gather_second(gather_first(x, n, what), n, what) for x in (own_in, own_out)
            )
        own_out = jnp.pad(own_out, ((0, 0), (0, width_in - width_d)))
        both = jnp.concatenate([own_in, own_out], axis=0)
        with jax.named_scope(what):
            return both, swap(both, "dp", 1, n), swap(both, "dp", 2, n)

    def owned_second(state, what, later=None):
        if n != 4:
            return state if later is None else (state, later)
        own, first, second = state
        half = own.shape[0] // 2
        with jax.named_scope(what):
            items = first[:half], second[half:]
            if later is not None:
                *items, later = tie(*items, later)
            low = swap(items[0], "dp", 2, n)
            high = swap(items[1], "dp", 1, n)
        out = [own, first, second, jnp.concatenate([low, high], axis=0)], None
        return out if later is None else (out, later)

    def finished_layer(layer, owned, before):
        parts, apart = owned
        gain = norm_gain[layer].astype(F32)
        *buffers, norm, norm_row = finish(
            layer,
            shift,
            parts,
            apart,
            input_proj,
            step_proj,
            gain,
            out_part,
            width_d,
            before,
            cd,
            inner,
        )
        return buffers, norm[:, 0] + norm_row[0]

    def small_rows(*sums):
        rows = jnp.concatenate(
            [jnp.concatenate(sums[2 * l : 2 * l + 2], axis=1) for l in range(layers)]
        )
        return jnp.pad(rows, ((0, 0), (0, width_d - rows.shape[1]))).astype(BF)

    def small_owned(parts):
        parts = [part.reshape(layers, 8, part.shape[1]) for part in parts]
        f = 2 * z + core

        def mine(x, width):
            return lax.dynamic_slice_in_dim(x, f * width, width, x.ndim - 1)

        conv = jnp.concatenate(
            [part[:, :5, :cd] for part in parts]
            + [sum(part[:, :5, cd:conv_ch] for part in parts)],
            axis=2,
        )
        conv = mine(conv, conv_f)
        gain = mine(jnp.concatenate([part[:, 6, :cd] for part in parts], axis=1), gate_f)
        skip = jnp.concatenate([part[:, 5, :cd] for part in parts], axis=1)
        skip = mine(jnp.sum(skip.reshape(layers, heads, HEAD_DIM), axis=2), heads_f)
        at = slice(conv_ch, conv_ch + hd)
        both = mine(jnp.concatenate([part[:, :2, at] for part in parts], axis=2), heads_f)
        return conv[:, :4], conv[:, 4], both[:, 0], both[:, 1], skip, gain

    both = lax.ppermute(
        doc_lengths,
        ("dp", "z"),
        [(i * z_count + j, j * z_count + i) for i in range(n) for j in range(z_count)],
    )
    ends = jnp.cumsum(pick(both, core))
    tok = hidden_in.shape[1]
    block_rows = 2 * tok
    row_len = block_rows * z_count
    q = block_rows // n
    positions = jnp.arange(row_len, dtype=jnp.int32)
    begin = jnp.max(jnp.where(ends[None, :] <= positions[:, None], ends[None, :], 0), axis=1)
    age = (positions - begin).reshape(z_count, block_rows)
    follow = jnp.concatenate([age[1:, :HALO], jnp.zeros((1, HALO), jnp.int32)], axis=0)
    age = jnp.concatenate([age, follow], axis=1)[:, :, None]

    def normalize(resid):
        inv = lax.rsqrt(jnp.mean(resid * resid, axis=-1, keepdims=True) + EPSILON)
        return inv, resid * inv

    def flat(x):
        return x.reshape(-1, x.shape[-1])

    both = both_cores(hidden_in, "hidden_cores")
    small = (
        conv_weight.reshape(layers * 4, conv_f),
        conv_bias,
        gate_gain,
        step_bias,
        decay_log,
        skip_gain,
    )
    shard0 = weight_shard(
        shift, 0, input_proj, step_proj, norm_gain[0].astype(F32), cd, hd, small
    )
    column0 = lax.all_gather(shard_out(0), PLANE)
    both, shard0 = tie(both, shard0)
    w_in0 = lax.all_gather(shard0, PLANE)
    groups = to_groups(both, n, "hidden_groups")
    resid0 = to_chunks(groups, z_count, "hidden_chunks").astype(F32)
    inv0, unit = normalize(resid0)
    unit = unit.astype(BF)
    shard1 = weight_shard(shift, 1, input_proj, step_proj, norm_gain[1].astype(F32), cd, hd)
    shard1, shard_out1, unit, column0 = tie(shard1, shard_out(1), unit, column0)
    w_in1 = lax.all_gather(shard1, PLANE)
    state = gather_first(unit, n, "unit0")
    parts = moved(column_sends(column0), "dp", "weight_out0")
    state, parts, cot = tie(state, parts, cotangent)
    units0 = gather_second(state, n, "unit0")
    w_out0 = weight_out(parts)
    cot_both = both_cores(cot, "cot_cores")
    cot_groups = moved(sends(cot_both.reshape(n, q, width_d), d, n), "dp", "cot_groups")
    pcs, phs = small_unpack(w_in0[:, d_rows:, :small_lanes])

    unit_cat0, mixed0, gated0, pre0, ssd0, states0, *sent = mixer_forward(
        shift, units0, w_in0, w_out0, age, pcs[0], phs[0]
    )
    sent, cot_groups, shard_out1 = tie(sent, cot_groups, shard_out1)
    state = reduce_first(sent, n, "product0")
    cot_chunks = moved(sends(jnp.stack(cot_groups), z ^ d, z_count), "z", "cot_chunks")
    state, shard_out1 = tie(state, shard_out1)
    terms = reduce_second(state, n, "product0")
    piece1 = to_slices(shard_out1, "weight_out1")
    terms, cot_chunks = tie_terms(terms, cot_chunks)
    resid1, branch0, ginv0, inv1, unit = settle_forward(terms, resid0, inner)

    state = gather_first(unit, n, "unit1")
    piece1, state = tie(piece1, state)
    w_out1 = lax.all_gather(piece1, PLANE).reshape(cd, width_d)
    units1 = gather_second(state, n, "unit1")
    cot_chunks, units1, w_in1 = tie(cot_chunks, units1, w_in1)
    upstream = jnp.stack(cot_chunks)
    state = gather_first(upstream, n, "upstream")
    unit_cat1, mixed1, gated1, pre1, ssd1, states1, sums1 = mixer_forward(
        shift, units1, w_in1, None, age, pcs[1], phs[1]
    )
    state, gated1, sums1 = tie(state, gated1, sums1)
    upstream_parts = gather_second(state, n, "upstream")

    def summed(totals, what):
        shape = totals.shape
        totals = totals.reshape(-1, row_len // LANES, LANES)
        bit = 1
        while bit < n:
            with jax.named_scope(what):
                totals = totals + swap(totals, "dp", bit, n)
            bit *= 2
        return totals.reshape(shape)

    s1 = summed(jnp.sum(sums1.astype(F32), axis=-1), "sum1")
    ginv1 = lax.rsqrt(s1 / inner + EPSILON)
    upstream_parts = joined(upstream_parts)
    upstream_all = place(shift, upstream_parts, 0)
    gg1 = mm_bt(flat(upstream_all), w_out1).reshape(n, z_count, q, cd)
    s2 = jnp.sum(gg1 * gated1.astype(F32), axis=-1)
    weighted, s2 = tie((gated1.astype(F32) * ginv1[..., None]).astype(BF), s2)
    d_out1 = mm_at(flat(weighted), flat(upstream_all)).astype(BF)
    sent1 = mm(flat(after(gated1, s2)), w_out1).astype(BF).reshape(n, z_count, q, width_d)
    s2, d_out1, sent1 = tie(summed(s2, "sum2"), d_out1, sent1)
    scales = jnp.stack([ginv1, ginv1 * ginv1 * ginv1 * s2 / inner], axis=-1)
    own = pick(ginv1, d)[..., None]

    total1 = lax.psum_scatter(sent1, "dp", scatter_dimension=0)
    sum_out1 = grad_out_sum(d_out1)
    d_mixed, wide_sums1, head_sums1, *sent = mixer_backward(
        shift,
        gg1,
        scales,
        None,
        w_in1,
        mixed1,
        age,
        pcs[1],
        phs[1],
        pre1,
        ssd1,
        states1,
        width_d,
    )
    total1, sent = tie(total1, sent)
    state = reduce_first(sent, n, "back1")
    hidden_out = (resid1 + total1.astype(F32) * own).astype(BF)
    out_chunks = moved([hidden_out[k] for k in range(z_count)], "z", "hidden_out_chunks")
    d_in1 = grad_in(*after((unit_cat1, d_mixed), sent))
    state, d_in1 = tie(state, d_in1)
    own_in1 = lax.psum_scatter(d_in1, PLANE, scatter_dimension=0, tiled=True)
    terms = reduce_second(state, n, "back1")
    back1, payload = settle_backward(terms, resid1, inv1, upstream, inner, branch0, ginv0)

    payload, sum_out1 = tie(payload, sum_out1)
    own_out1 = to_owners(sum_out1, "grad_out1")
    g_all = gather_second(gather_first(payload, n, "branch_grad0"), n, "branch_grad0")
    d_out0 = mm_at(flat(gated0), flat(jnp.stack(joined(g_all)))[:, :width_d]).astype(BF)
    items, g_all = tie(grad_out_sends(d_out0), g_all)
    by_rows = moved(items, "dp", "grad_out0")
    d_mixed, wide_sums0, head_sums0, *sent = mixer_backward(
        shift,
        g_all,
        None,
        w_out0,
        w_in0,
        mixed0,
        age,
        pcs[0],
        phs[0],
        pre0,
        ssd0,
        states0,
        width_d,
    )
    own_in1, own_out1, by_rows, sent, out_chunks = tie(
        own_in1, own_out1, by_rows, sent, out_chunks
    )
    state = reduce_first(sent, n, "back0")
    own_out0 = grad_out_owned(by_rows)
    d_in0 = grad_in(*after((unit_cat0, d_mixed), sent))
    sums = small_rows(wide_sums0, head_sums0, wide_sums1, head_sums1)
    state, d_in0, sums = tie(state, d_in0, sums)
    own_in0 = lax.psum_scatter(d_in0, PLANE, scatter_dimension=0, tiled=True)
    terms = reduce_second(state, n, "back0")
    terms, (own_in1, own_out1) = tie_terms(terms, (own_in1, own_out1))
    (back0,) = settle_backward(terms, resid0, inv0, back1, inner)

    items = [jnp.concatenate([back0[k], sums], axis=0) for k in range(z_count)]
    chunks = moved(items, "z", "back_chunks")
    first = owned_first(*after((own_in1, own_out1), items), "owned1")
    chunks, first = tie(chunks, first)
    sums = sum(chunk[q:].astype(F32) for chunk in chunks).astype(BF)
    both = jnp.stack(
        [jnp.concatenate([x[:q], y], axis=1) for x, y in zip(chunks, out_chunks)]
    )
    sums = jnp.pad(sums, ((0, 0), (0, width_d)))
    items = [jnp.concatenate([item, sums], axis=0) for item in sends(both, z ^ d, n)]
    groups = moved(items, "dp", "back_groups")
    owned1 = owned_second(after(first, items), "owned1")
    groups, owned1, own_in0, own_out0 = tie(groups, owned1, own_in0, own_out0)
    buffers, norm1 = finished_layer(1, owned1, None)
    first = owned_first(own_in0, own_out0, "owned0")
    results, sums = from_both(groups, q, "back_cores")
    first, results, buffers = tie(first, results, buffers)
    owned0, sums = owned_second(first, "owned0", sums)
    hidden_grad = results[..., :width_d].astype(F32)
    hidden_out = results[..., width_d:]
    smalls = small_owned(sums)
    owned0, hidden_grad, hidden_out, smalls = tie(owned0, hidden_grad, hidden_out, smalls)
    buffers, norm0 = finished_layer(0, owned0, buffers)
    norm = jnp.stack([norm0, norm1])
    conv_grad, conv_bias_grad, bias_grad, decay_grad, skip_grad, gain_grad = smalls
    return (
        hidden_out,
        hidden_grad,
        norm,
        buffers[0],
        buffers[2],
        conv_grad,
        conv_bias_grad,
        bias_grad,
        decay_grad,
        skip_grad,
        gain_grad,
        buffers[1],
    )


def solution(mesh):
    n = mesh.shape["dp"]
    z_count = mesh.shape["fsdp"] // 2
    assert n == z_count
    split = Mesh(mesh.devices.reshape(n, z_count, 2), ("dp", "z", "core"))
    fsdp = PLANE
    tokens = P("dp", fsdp, None)
    last = P(None, fsdp)
    weights = (
        last,
        P(None, fsdp, None),
        P(None, None, fsdp),
        P(None, None, fsdp),
        last,
        last,
        last,
        last,
        last,
        P(None, fsdp, None),
    )
    return jax.shard_map(
        partial(on_device, n=n, z_count=z_count),
        mesh=split,
        in_specs=(tokens, P("dp", None)) + weights + (tokens,),
        out_specs=(tokens, tokens) + weights,
        check_vma=False,
    )
```
